32 devices in a mesh: groups: 2 (over x), tile: 16 (over z, y, core).
Axes of the slice: x: 2, y: 2, z: 4, core: 2. Of those that a mesh axis runs over, the one named last changes fastest.
Arguments:
- data_halves: bfloat16 [2, 4, 256, 32, 512], P(None, None, ('groups', 'tile')), parts along dimension 2, may hold values from 0.1 to 20, as said below
- psf_taps: float32 [4, 3, 9], replicated, may hold values from 0.05 to 1
- cycle_map: int32 [32, 32, 512], P(('groups', 'tile')), parts along dimension 0, may hold values from 0 to 255, as said below
- cutoff: int32 [2], P('groups'), parts along dimension 0, may hold values from 64 to 255
Outputs:
- joined: float32 [256, 32, 512], P(('groups', 'tile')), parts along dimension 0
The draws below stay inside these ranges and needn't reach their ends.
There are 2 independent parts, one for each index of `groups`. The reference program is written for one: setup_inputs(seed, part) draws one part's arguments, and reference() takes and returns one part's arrays. A program takes and returns all parts, laid end to end along the dimension named above; an argument that names none is the same for every part. Nothing has to cross between parts.
Inputs may be any that keep to these rules, and one draw needn't show every extreme that they name: `data_halves`: positive photon counts. cycle_map[b, k, l] is the cycle of frequency (k, l) in block b: with fk = min(k, 32 - k), fl = min(l, 512 - l) and a whole stretch s_b of 1 to 4 drawn for each block, the largest r with r * r <= (s_b fk)^2 + fl^2, capped at 255.
All inputs are finite; a program needn't handle non-finite values.
Results may differ from the reference program's by a relative error of at most 0.00095.
The reference program's roundings to bfloat16 on the way count: a program that leaves them out, or rounds other values in their place, can miss the bound.
Values may be sent and summed in bfloat16 or wider, within the bound.
A program may use at most 64 MiB of HBM per device.

```python
import math
import jax
import jax.numpy as jnp
from jax import lax

SLAB = 8
DEPTH = 32
LATERAL = 512
VIEWS = 4
TAPS = 9
ITERS = 2
CYCLES = 256
BLOCKS = 16
EXTENT = 128


def draw_data_halves(key, part):
    key_signal, key_noise, key_place = jax.random.split(jax.random.fold_in(key, 11), 3)
    position = jnp.arange(EXTENT).astype(jnp.float32) / EXTENT
    profile = jnp.exp(jnp.log(4.0) * position)[:, None, None]
    signal = jnp.clip(jnp.exp(0.4 * jax.random.normal(key_signal, (EXTENT, DEPTH, LATERAL), jnp.float32)), 0.2, 3.0)
    quarter = jax.random.randint(key_place, (), 1, 4)
    row_quarter = jnp.arange(EXTENT) * 4 // EXTENT
    strength = jnp.where(row_quarter == quarter, 0.5, 0.05).astype(jnp.float32)
    unit_noise = jax.random.uniform(key_noise, (2, VIEWS, EXTENT, DEPTH, LATERAL), jnp.float32, -1.0, 1.0)
    shot_noise = 1.0 + strength[None, None, :, None, None] * unit_noise
    return (profile * signal * shot_noise).astype(jnp.bfloat16)


def draw_cycle_map(key, part):
    stretch = jax.random.randint(jax.random.fold_in(key, 23), (BLOCKS,), 1, 5)
    index_z = jnp.arange(DEPTH)
    index_y = jnp.arange(LATERAL)
    fold_z = jnp.minimum(index_z, DEPTH - index_z)
    fold_y = jnp.minimum(index_y, LATERAL - index_y)
    scaled = stretch[:, None] * fold_z[None, :]
    radius_sq = scaled[:, :, None] ** 2 + (fold_y ** 2)[None, None, :]
    lowest = jnp.zeros_like(radius_sq)
    for bit_number in range(12, -1, -1):
        candidate = lowest + (1 << bit_number)
        lowest = jnp.where(candidate * candidate <= radius_sq, candidate, lowest)
    cycle = jnp.minimum(lowest, CYCLES - 1)
    return cycle.astype(jnp.int32)


def setup_inputs(seed: int = 0, part: int = 0) -> dict:
    seeds = jax.random.split(jax.random.key(seed), 5)
    own_keys = jax.random.split(jax.random.fold_in(seeds[4], part), 5)
    return {
        "data_halves": draw_data_halves(jax.random.fold_in(jax.random.fold_in(seeds[4], part), 71), part),
        "psf_taps": jnp.clip(jnp.exp(jax.random.uniform(seeds[1], (VIEWS, 3, TAPS), jnp.float32, math.log(0.05), math.log(1.0))), 0.05, 1.0),
        "cycle_map": draw_cycle_map(jax.random.fold_in(jax.random.fold_in(seeds[4], part), 71), part),
        "cutoff": jax.random.randint(own_keys[3], (1,), CYCLES // 4, CYCLES).astype(jnp.int32),
    }


highest = lax.Precision.HIGHEST

def conv_axis(volume, kernel, along):
    radius = kernel.shape[-1] // 2
    length = volume.shape[along]
    widths = [(0, 0)] * volume.ndim
    widths[along] = (radius, radius)
    padded = jnp.pad(volume, widths)
    summed = jnp.zeros_like(volume)
    for tap_index in range(kernel.shape[-1]):
        shifted = lax.slice_in_dim(padded, tap_index, tap_index + length, axis=along)
        summed = summed + kernel[:, tap_index][:, None, None, None] * shifted
    return summed

def blur_field(volume, kernels):
    volume = conv_axis(volume, kernels[:, 0], 1)
    volume = conv_axis(volume, kernels[:, 1], 2)
    return conv_axis(volume, kernels[:, 2], 3)

def tables(length):
    index_n = jnp.arange(length)
    phase = index_n[:, None] * index_n[None, :] % length
    angle = phase.astype(jnp.float32) * (2.0 * jnp.pi / length)
    return (jnp.cos(angle), jnp.sin(angle))

def reference(data_halves, psf_taps, cycle_map, cutoff):
    kernels = psf_taps / lax.optimization_barrier(jnp.sum(psf_taps, axis=-1, keepdims=True))
    mirrored = kernels[:, :, ::-1]
    cos_z, sin_z = tables(DEPTH)
    cos_full, sin_full = tables(LATERAL)
    lat_cos = cos_full.astype(jnp.bfloat16)
    lat_sin = sin_full.astype(jnp.bfloat16)
    reals = []
    imags = []
    for half_index in range(2):
        observed = data_halves[half_index].astype(jnp.float32)
        estimate = lax.optimization_barrier(jnp.mean(observed, axis=0))
        for iteration in range(ITERS):
            predicted = blur_field(jnp.broadcast_to(estimate[None], observed.shape), kernels)
            correction = blur_field(observed / predicted, mirrored)
            estimate = estimate * lax.optimization_barrier(jnp.mean(correction, axis=0))
        rounded = estimate.astype(jnp.bfloat16).reshape(-1, LATERAL)
        row_real = jnp.dot(rounded, lat_cos, preferred_element_type=jnp.float32).reshape(EXTENT, DEPTH, LATERAL)
        row_imag = -jnp.dot(rounded, lat_sin, preferred_element_type=jnp.float32).reshape(EXTENT, DEPTH, LATERAL)
        spec_real = jnp.einsum('kz,xzl->xkl', cos_z, row_real, precision=highest) + jnp.einsum('kz,xzl->xkl', sin_z, row_imag, precision=highest)
        spec_imag = jnp.einsum('kz,xzl->xkl', cos_z, row_imag, precision=highest) - jnp.einsum('kz,xzl->xkl', sin_z, row_real, precision=highest)
        reals.append(spec_real)
        imags.append(spec_imag)
    cross_power = reals[0] * reals[1] + imags[0] * imags[1]
    power_a = reals[0] ** 2 + imags[0] ** 2
    power_b = reals[1] ** 2 + imags[1] ** 2
    cycle_ids = cycle_map.reshape(-1)

    def cycle_total(values):
        per_block = lax.optimization_barrier(jnp.sum(values.reshape(BLOCKS, SLAB, DEPTH, LATERAL), axis=1))
        return jax.ops.segment_sum(per_block.reshape(-1), cycle_ids, CYCLES)
    numerator = cycle_total(cross_power)
    cycle_corr = numerator / (jnp.sqrt(cycle_total(power_a)) * jnp.sqrt(cycle_total(power_b)))
    cycle_weight = jnp.where(jnp.arange(CYCLES) <= cutoff[0], cycle_corr, 0.0)
    cell_weight = cycle_weight[cycle_map][:, None]
    mixed_real = ((0.5 * (reals[0] + reals[1])).reshape(BLOCKS, SLAB, DEPTH, LATERAL) * cell_weight).reshape(EXTENT, DEPTH, LATERAL)
    mixed_imag = ((0.5 * (imags[0] + imags[1])).reshape(BLOCKS, SLAB, DEPTH, LATERAL) * cell_weight).reshape(EXTENT, DEPTH, LATERAL)
    inner_real = jnp.einsum('zk,xkl->xzl', cos_z, mixed_real, precision=highest) - jnp.einsum('zk,xkl->xzl', sin_z, mixed_imag, precision=highest)
    inner_imag = jnp.einsum('zk,xkl->xzl', sin_z, mixed_real, precision=highest) + jnp.einsum('zk,xkl->xzl', cos_z, mixed_imag, precision=highest)
    inner_real = inner_real.astype(jnp.bfloat16).reshape(-1, LATERAL)
    inner_imag = inner_imag.astype(jnp.bfloat16).reshape(-1, LATERAL)
    joined = jnp.dot(inner_real, lat_cos, preferred_element_type=jnp.float32) - jnp.dot(inner_imag, lat_sin, preferred_element_type=jnp.float32)
    joined = joined.reshape(EXTENT, DEPTH, LATERAL) / (DEPTH * LATERAL)
    return joined.astype(jnp.float32)
```

```python
import functools

import jax
import jax.numpy as jnp
import ml_dtypes
import numpy as np
from jax import lax
from jax.experimental import pallas as pl
from jax.experimental.pallas import tpu as pltpu
from jax.sharding import PartitionSpec as P

ITERS = 2
CYCLES = 256
MESH = pl.DeviceIdType.MESH
F32 = jnp.float32
BF16 = jnp.bfloat16


def cos_sin(length):
    index_n = np.arange(length)
    phase = index_n[:, None] * index_n[None, :] % length
    angle = phase.astype(np.float32) * np.float32(2.0 * np.pi / length)
    return np.cos(angle).astype(np.float32), np.sin(angle).astype(np.float32)


def split_np(matrix):
    high = matrix.astype(ml_dtypes.bfloat16)
    low = (matrix - high.astype(np.float32)).astype(ml_dtypes.bfloat16)
    return np.concatenate([high, low, high], axis=1)


def constants(depth, lateral):
    half = depth // 2
    order = np.concatenate([np.arange(half + 1), depth - np.arange(1, half)])
    cos_z, sin_z = cos_sin(depth)
    cos_z, sin_z = cos_z[order], sin_z[order]
    eye = np.eye(128 // depth, dtype=np.float32)
    cos_k, sin_k = np.kron(eye, cos_z), np.kron(eye, sin_z)
    forward = np.block([[cos_k, sin_k], [-sin_k, cos_k]])
    inverse = np.ascontiguousarray(forward.T)
    cos_y, sin_y = cos_sin(lateral)
    lateral_table = np.concatenate([cos_y, -sin_y], axis=1).astype(ml_dtypes.bfloat16)
    return lateral_table, split_np(forward), split_np(inverse)


def split(value):
    high = value.astype(BF16)
    low = (value - high.astype(F32)).astype(BF16)
    return high, low


def dot(a, b):
    return lax.dot_general(a, b, (((1,), (0,)), ((), ())), preferred_element_type=F32)


def kernel(
    n, data, psf, cycles, cutoff, table, forward_z, inverse_z, out,
    est, halo, corr_out, corr_in, corr_own, spread, gather, lat_f, lat_b,
    dext, first, cs, onehot, spec, folded, red_out, red_in,
    halo_send, halo_recv, corr_send, corr_recv, red_send, red_recv,
):
    me = lax.axis_index("tile")
    has_left = me > 0
    has_right = me < n - 1

    barrier = pltpu.get_barrier_semaphore()

    def greet(step, carry):
        peer = lax.rem(me + step, n)
        pl.semaphore_signal(barrier, inc=1, device_id={"tile": peer}, device_id_type=MESH)
        return carry

    lax.fori_loop(1, n, greet, 0)

    for h in range(2):
        total = data[h, 0].astype(F32)
        for v in range(1, 4):
            total = total + data[h, v].astype(F32)
        est[h] = total * 0.25

    pl.semaphore_wait(barrier, n - 1)

    def halo_copy(it, h, side):
        peer = lax.rem(me + n - 1, n) if side == 0 else lax.rem(me + 1, n)
        return pltpu.make_async_remote_copy(
            src_ref=est.at[h, pl.ds(128 * side, 128)],
            dst_ref=halo.at[it, h, 1 - side],
            send_sem=halo_send.at[it, h, side],
            recv_sem=halo_recv.at[it, h, 1 - side],
            device_id={"tile": peer},
            device_id_type=MESH,
        )

    def corr_copy(it, h, side):
        peer = lax.rem(me + n - 1, n) if side == 0 else lax.rem(me + 1, n)
        return pltpu.make_async_remote_copy(
            src_ref=corr_out.at[it, h, side],
            dst_ref=corr_in.at[it, h, 1 - side],
            send_sem=corr_send.at[it, h, side],
            recv_sem=corr_recv.at[it, h, 1 - side],
            device_id={"tile": peer},
            device_id_type=MESH,
        )

    def on_side(side, action):
        pl.when(has_left if side == 0 else has_right)(action)

    def start(make, it, h):
        for side in range(2):
            on_side(side, lambda: make(it, h, side).start())

    def wait_recv(make, it, h):
        for side in range(2):
            on_side(side, lambda: make(it, h, 1 - side).wait_recv())

    def wait_send(make, it, h):
        for side in range(2):
            on_side(side, lambda: make(it, h, side).wait_send())

    start(halo_copy, 0, 0)
    start(halo_copy, 0, 1)

    def clear(side):
        for it in range(ITERS):
            for h in range(2):
                halo[it, h, side] = jnp.zeros((128, halo.shape[-1]), F32)
                corr_in[it, h, side] = jnp.zeros((128, halo.shape[-1]), F32)

    pl.when(jnp.logical_not(has_left))(lambda: clear(0))
    pl.when(jnp.logical_not(has_right))(lambda: clear(1))

    row = lax.broadcasted_iota(jnp.int32, (128, 128), 0)
    col = lax.broadcasted_iota(jnp.int32, (128, 128), 1)
    depth = data.shape[2] // 8
    shift_y = row - col + 4
    shift_z = col % depth - row % depth + 4
    shift_x = col // depth - row // depth

    def taps_of(v, axis):
        taps = [psf[v, axis, t] for t in range(9)]
        total = taps[0]
        for t in range(1, 9):
            total = total + taps[t]
        return taps, jnp.ones((128, 128), F32) / jnp.full((128, 128), total, F32)

    def select(shift, taps, low, high):
        value = jnp.zeros((128, 128), F32)
        for t in range(low, high):
            value = jnp.where(shift == t, taps[t], value)
        return value

    zero = jnp.zeros((128, 128), BF16)

    def build(v, carry):
        for mirrored in range(2):
            (kx, nx), (ky, ny), (kz, nz) = taps_of(v, 0), taps_of(v, 2), taps_of(v, 1)
            if mirrored:
                kx, ky, kz = kx[::-1], ky[::-1], kz[::-1]
            band_z = select(shift_z, kz, 0, 9) * (nx * nz)
            at_v = pl.ds(pl.multiple_of(v * 128, 128), 128)
            for s in range(3):
                low, high = split(select(shift_x + 4 * s, kx, max(4 * s - 3, 0), min(4 * s + 4, 9)) * band_z)
                for part, value in enumerate((low, high, low)):
                    if mirrored:
                        column = pl.ds(pl.multiple_of(v * 384 + part * 128, 128), 128)
                        gather[pl.ds(256 - 128 * s, 128), column] = value
                    else:
                        spread[at_v, pl.ds(384 * s + 128 * part, 128)] = value
            lat = lat_b if mirrored else lat_f
            same = split(select(shift_y, ky, 0, 9) * ny)
            after = split(select(shift_y + 128, ky, 0, 4 + 5) * ny)
            before = split(select(shift_y - 128, ky, 0, 9) * ny)
            for part, which in enumerate((0, 1, 0)):
                for b in range(2):
                    for i in range(3):
                        for o in range(2):
                            step = (i + b) - (o + 2 * b)
                            value = {0: same, 1: after, -1: before}.get(step)
                            value = zero if value is None else value[which]
                            lat[v, b, pl.ds(384 * part + 128 * i, 128), pl.ds(128 * o, 128)] = value
        return carry

    lax.fori_loop(0, 4, build, 0)

    bins = lax.broadcasted_iota(jnp.int32, (CYCLES, 256), 0)

    def mark(k, carry):
        ids = cycles[0, pl.ds(k, 1), pl.ds(0, 256)]
        onehot[k] = jnp.where(bins == ids, 1.0, 0.0).astype(BF16)
        return carry

    lax.fori_loop(0, depth // 2 + 1, mark, 0)

    def put_parts(ref, base, value):
        high, low = split(value)
        ref[pl.ds(base, 128)] = high
        ref[pl.ds(base + 128, 128)] = high
        ref[pl.ds(base + 256, 128)] = low

    def along_y(value, lat, v):
        high, low = split(value)
        for b in range(2):
            at = slice(128 * b, 128 * b + 384)
            lhs = jnp.concatenate([high[:, at], high[:, at], low[:, at]], axis=1)
            yield dot(lhs, lat[v, b])

    def sweep(it, h):
        put_parts(dext, 0, halo[it, h, 0])
        put_parts(dext, 384, est[h, pl.ds(0, 128)])
        put_parts(dext, 768, est[h, pl.ds(128, 128)])
        put_parts(dext, 1152, halo[it, h, 1])
        for i in range(2):
            first[i] = dot(spread[...], dext[pl.ds(384 * i, 1152)])

        def view(v, carry):
            at_v = pl.ds(pl.multiple_of(v * 128, 128), 128)
            value = jnp.concatenate([first[0, at_v], first[1, at_v]], axis=0)
            quotient = [
                data[h, v, :, pl.ds(256 * b, 256)].astype(F32) / predicted
                for b, predicted in enumerate(along_y(value, lat_f, v))
            ]
            quotient = jnp.concatenate(quotient, axis=1)
            for b, corrected in enumerate(along_y(quotient, lat_b, v)):
                high, low = split(corrected)
                for part, piece in enumerate((high, high, low)):
                    at = pl.ds(pl.multiple_of(v * 384 + 128 * part, 128), 128)
                    for side in range(2):
                        cs[side, at, pl.ds(256 * b, 256)] = piece[128 * side : 128 * side + 128]
            return carry

        lax.fori_loop(0, 4, view, 0)
        r0 = dot(gather[...], cs[0])
        corr_out[it, h, 0] = r0[:128]
        corr_own[h] = r0[128:]
        r1 = dot(gather[...], cs[1])
        corr_out[it, h, 1] = r1[256:]
        corr_own[h] += r1[:256]

    def update(it, h):
        wait_send(halo_copy, it, h)
        wait_recv(corr_copy, it, h)
        for side in range(2):
            at = pl.ds(128 * side, 128)
            est[h, at] = est[h, at] * (0.25 * (corr_own[h, at] + corr_in[it, h, side]))

    def spectrum(h):
        rows = dot(est[h].astype(BF16), table[...])
        lateral = rows.shape[1] // 2
        for g in range(2):
            at = slice(128 * g, 128 * g + 128)
            both = jnp.concatenate([rows[at, :lateral], rows[at, lateral:]], axis=0)
            high, low = split(both)
            spec[h, g] = dot(forward_z[...], jnp.concatenate([high, high, low], axis=0))

    for it in range(ITERS):
        for h in range(2):
            wait_recv(halo_copy, it, h)
            sweep(it, h)
            start(corr_copy, it, h)
        for h in range(2):
            update(it, h)
            if it + 1 < ITERS:
                start(halo_copy, it + 1, h)
            else:
                spectrum(h)

    lateral = data.shape[3]
    half = depth // 2

    def power(a, b):
        total = jnp.zeros((depth, lateral), F32)
        for g in range(2):
            for at in range(0, 256, depth):
                total = total + spec[a, g, pl.ds(at, depth)] * spec[b, g, pl.ds(at, depth)]
        return total

    lane = lax.broadcasted_iota(jnp.int32, (1, 256), 1)
    weight_l = jnp.where(lane == 0, 1.0, 2.0)
    rows16 = lax.broadcasted_iota(jnp.int32, (half, 256), 0)
    folded[...] = jnp.zeros_like(folded)
    edge = []
    for q, (a, b) in enumerate(((0, 1), (0, 0), (1, 1))):
        total = power(a, b)
        edge.append(jnp.sum(total[:, 256:257], axis=0, keepdims=True))
        low = total[:half, :256]
        high = total[half:, :256]
        pairs = (low + jnp.where(rows16 == 0, 0.0, high)) * weight_l
        last = high[:1] * weight_l
        for k in range(half):
            folded[k, q : q + 1] = pairs[k : k + 1]
        folded[half, q : q + 1] = last

    binned = jnp.zeros((32, CYCLES), F32)
    for k in range(half + 1):
        value = folded[k]
        a = value.astype(BF16).astype(F32)
        b = (value - a).astype(BF16).astype(F32)
        c = value - a - b
        lhs = jnp.concatenate([a, b, c, jnp.zeros_like(a)], axis=0).astype(BF16)
        binned = binned + lax.dot_general(
            lhs, onehot[k], (((1,), (1,)), ((), ())), preferred_element_type=F32
        )
    binned = binned[0:8] + binned[8:16] + binned[16:24]
    bin_row = lax.broadcasted_iota(jnp.int32, (8, CYCLES), 0)
    bin_lane = lax.broadcasted_iota(jnp.int32, (8, CYCLES), 1)
    for q in range(3):
        binned = binned + jnp.where(
            (bin_row == q) & (bin_lane == CYCLES - 1), jnp.broadcast_to(edge[q], (8, CYCLES)), 0.0
        )
    red_out[...] = binned

    def share(step):
        peer = lax.rem(me + step, n)
        return pltpu.make_async_remote_copy(
            src_ref=red_out,
            dst_ref=red_in.at[step],
            send_sem=red_send.at[step],
            recv_sem=red_recv.at[step],
            device_id={"tile": peer},
            device_id_type=MESH,
        )

    def start_share(step, carry):
        share(step).start()
        return carry

    def wait_share(step, carry):
        share(step).wait()
        return carry + red_in[step]

    lax.fori_loop(1, n, start_share, 0)
    totals = lax.fori_loop(1, n, wait_share, binned)

    corr = totals[0:1] / (jnp.sqrt(totals[1:2]) * jnp.sqrt(totals[2:3]))
    scale = 0.5 / (depth * lateral)
    cycle_weight = jnp.where(lane <= cutoff[0], corr, 0.0) * scale
    low_table = jnp.broadcast_to(cycle_weight[:, :128], (8, 128))
    high_table = jnp.broadcast_to(cycle_weight[:, 128:], (8, 128))
    weights = []
    for r in range(0, half + 8, 8):
        pieces = []
        for c in range(0, lateral, 128):
            ids = cycles[0, pl.ds(r, 8), pl.ds(c, 128)]
            index = ids & 127
            from_low = jnp.take_along_axis(low_table, index, axis=1)
            from_high = jnp.take_along_axis(high_table, index, axis=1)
            pieces.append(jnp.where(ids < 128, from_low, from_high))
        weights.append(jnp.concatenate(pieces, axis=1))
    low = jnp.concatenate(weights[:-1], axis=0)
    row0 = lax.broadcasted_iota(jnp.int32, (half, lateral), 0) == 0
    high = jnp.where(row0, jnp.broadcast_to(weights[-1][0:1], (half, lateral)), low)
    cell = jnp.concatenate([low, high], axis=0)

    for g in range(2):
        mixed = jnp.concatenate(
            [
                (spec[0, g, pl.ds(at, depth)] + spec[1, g, pl.ds(at, depth)]) * cell
                for at in range(0, 256, depth)
            ],
            axis=0,
        )
        high, low = split(mixed)
        inner = dot(inverse_z[...], jnp.concatenate([high, high, low], axis=0)).astype(BF16)
        out[pl.ds(128 * g, 128)] = dot(inner[:128], table[:, pl.ds(0, lateral)]) + dot(
            inner[128:], table[:, pl.ds(lateral, lateral)]
        )

    for it in range(ITERS):
        for h in range(2):
            wait_send(corr_copy, it, h)


def body(data_halves, psf_taps, cycle_map, cutoff):
    halves, views, slab, depth, lateral = data_halves.shape
    n = lax.axis_size("tile")
    rows = slab * depth
    table, forward_z, inverse_z = constants(depth, lateral)
    vmem = pl.BlockSpec(memory_space=pltpu.VMEM)
    smem = pl.BlockSpec(memory_space=pltpu.SMEM)
    dma = pltpu.SemaphoreType.DMA
    joined = pl.pallas_call(
        functools.partial(kernel, n),
        out_shape=jax.ShapeDtypeStruct((rows, lateral), F32),
        in_specs=[vmem, smem, vmem, smem, vmem, vmem, vmem],
        out_specs=vmem,
        scratch_shapes=[
            pltpu.VMEM((2, rows, lateral), F32),
            pltpu.VMEM((ITERS, 2, 2, 128, lateral), F32),
            pltpu.VMEM((ITERS, 2, 2, 128, lateral), F32),
            pltpu.VMEM((ITERS, 2, 2, 128, lateral), F32),
            pltpu.VMEM((2, rows, lateral), F32),
            pltpu.VMEM((512, 1152), BF16),
            pltpu.VMEM((384, 1536), BF16),
            pltpu.VMEM((4, 2, 1152, 256), BF16),
            pltpu.VMEM((4, 2, 1152, 256), BF16),
            pltpu.VMEM((1536, lateral), BF16),
            pltpu.VMEM((2, 512, lateral), F32),
            pltpu.VMEM((2, 1536, lateral), BF16),
            pltpu.VMEM((depth // 2 + 1, CYCLES, 256), BF16),
            pltpu.VMEM((2, 2, rows, lateral), F32),
            pltpu.VMEM((depth // 2 + 1, 8, 256), F32),
            pltpu.VMEM((8, CYCLES), F32),
            pltpu.VMEM((n, 8, CYCLES), F32),
            dma((ITERS, 2, 2)),
            dma((ITERS, 2, 2)),
            dma((ITERS, 2, 2)),
            dma((ITERS, 2, 2)),
            dma((n,)),
            dma((n,)),
        ],
        compiler_params=pltpu.CompilerParams(
            collective_id=0, has_side_effects=True, vmem_limit_bytes=56 * 1024 * 1024
        ),
    )(
        data_halves.reshape(halves, views, rows, lateral),
        psf_taps,
        cycle_map,
        cutoff,
        jnp.asarray(table),
        jnp.asarray(forward_z),
        jnp.asarray(inverse_z),
    )
    return joined.reshape(slab, depth, lateral)


def solution(mesh):
    in_specs = (
        P(None, None, ("groups", "tile"), None, None),
        P(),
        P(("groups", "tile"), None, None),
        P("groups"),
    )
    out_specs = P(("groups", "tile"), None, None)
    return jax.shard_map(body, mesh=mesh, in_specs=in_specs, out_specs=out_specs, check_vma=False)
```

```python
import functools

import jax
import jax.numpy as jnp
import ml_dtypes
import numpy as np
from jax import lax
from jax.experimental import pallas as pl
from jax.experimental.pallas import tpu as pltpu
from jax.sharding import PartitionSpec as P

CYCLES = 256
MESH = pl.DeviceIdType.MESH
F32 = jnp.float32
BF16 = jnp.bfloat16


def cos_sin(length):
    index_n = np.arange(length)
    phase = index_n[:, None] * index_n[None, :] % length
    angle = phase.astype(np.float32) * np.float32(2.0 * np.pi / length)
    return np.cos(angle).astype(np.float32), np.sin(angle).astype(np.float32)


def split_np(matrix):
    high = matrix.astype(ml_dtypes.bfloat16)
    low = (matrix - high.astype(np.float32)).astype(ml_dtypes.bfloat16)
    return np.concatenate([high, low, high], axis=1)


def constants(depth, lateral):
    half = depth // 2
    order = np.concatenate([np.arange(half + 1), depth - np.arange(1, half)])
    cos_z, sin_z = cos_sin(depth)
    cos_z, sin_z = cos_z[order], sin_z[order]
    eye = np.eye(128 // depth, dtype=np.float32)
    cos_k, sin_k = np.kron(eye, cos_z), np.kron(eye, sin_z)
    forward = np.block([[cos_k, sin_k], [-sin_k, cos_k]])
    inverse = np.ascontiguousarray(forward.T)
    cos_y, sin_y = cos_sin(lateral)
    lateral_table = np.concatenate([cos_y, -sin_y], axis=1).astype(ml_dtypes.bfloat16)
    return lateral_table, split_np(forward), split_np(inverse)


def split(value):
    high = value.astype(BF16)
    low = (value - high.astype(F32)).astype(BF16)
    return high, low


def dot(a, b):
    return lax.dot_general(a, b, (((1,), (0,)), ((), ())), preferred_element_type=F32)


def kernel(
    n, data, psf, cycles, cutoff, table, forward_z, inverse_z, out,
    est, halo, corr_mine, corr_own, flat, both_out, both_in, last_out, last_in,
    spread, gather, lat_f, lat_b, dext, first, cs, onehot, spec, red_out, red_in,
    halo_send, halo_recv, both_send, both_recv, last_send, last_recv, red_send, red_recv,
):
    me = lax.axis_index("tile")
    has_left = me > 0
    has_right = me < n - 1

    barrier = pltpu.get_barrier_semaphore()

    def greet(step, carry):
        peer = lax.rem(me + step, n)
        pl.semaphore_signal(barrier, inc=1, device_id={"tile": peer}, device_id_type=MESH)
        return carry

    lax.fori_loop(1, n, greet, 0)

    def neighbour(side):
        return lax.rem(me + n - 1, n) if side == 0 else lax.rem(me + 1, n)

    def halo_copy(h, side):
        return pltpu.make_async_remote_copy(
            src_ref=est.at[h, pl.ds(128 * side, 128)],
            dst_ref=halo.at[h, 1 - side],
            send_sem=halo_send.at[h, side],
            recv_sem=halo_recv.at[h, 1 - side],
            device_id={"tile": neighbour(side)},
            device_id_type=MESH,
        )

    def both_copy(h, side):
        return pltpu.make_async_remote_copy(
            src_ref=both_out.at[h, side],
            dst_ref=both_in.at[h, 1 - side],
            send_sem=both_send.at[h, side],
            recv_sem=both_recv.at[h, 1 - side],
            device_id={"tile": neighbour(side)},
            device_id_type=MESH,
        )

    def last_copy(h, side):
        return pltpu.make_async_remote_copy(
            src_ref=last_out.at[h, side],
            dst_ref=last_in.at[h, 1 - side],
            send_sem=last_send.at[h, side],
            recv_sem=last_recv.at[h, 1 - side],
            device_id={"tile": neighbour(side)},
            device_id_type=MESH,
        )

    def on_side(side, action):
        pl.when(has_left if side == 0 else has_right)(action)

    def start(make, h):
        for side in range(2):
            on_side(side, lambda: make(h, side).start())

    def wait_recv(make, h):
        for side in range(2):
            on_side(side, lambda: make(h, 1 - side).wait_recv())

    def wait_send(make, h):
        for side in range(2):
            on_side(side, lambda: make(h, side).wait_send())

    for h in range(2):
        total = data[h, 0].astype(F32)
        for v in range(1, 4):
            total = total + data[h, v].astype(F32)
        est[h] = total * 0.25
        if h == 0:
            pl.semaphore_wait(barrier, n - 1)
        start(halo_copy, h)

    def clear(side):
        for h in range(2):
            halo[h, side] = jnp.zeros(halo.shape[2:], F32)
            both_in[h, side] = jnp.zeros(both_in.shape[2:], BF16)
            last_in[h, side] = jnp.zeros(last_in.shape[2:], last_in.dtype)

    pl.when(jnp.logical_not(has_left))(lambda: clear(0))
    pl.when(jnp.logical_not(has_right))(lambda: clear(1))

    row = lax.broadcasted_iota(jnp.int32, (128, 128), 0)
    col = lax.broadcasted_iota(jnp.int32, (128, 128), 1)
    depth = data.shape[2] // 8
    shift_y = row - col + 4
    shift_z = col % depth - row % depth + 4
    shift_x = col // depth - row // depth

    def taps_of(v, axis):
        taps = [psf[axis, v, t] for t in range(9)]
        total = taps[0]
        for t in range(1, 9):
            total = total + taps[t]
        return taps, jnp.ones((128, 128), F32) / jnp.full((128, 128), total, F32)

    def select(shift, taps, low, high):
        value = jnp.zeros((128, 128), F32)
        for t in range(low, high):
            value = jnp.where(shift == t, taps[t], value)
        return value

    zero = jnp.zeros((128, 128), BF16)

    def build(v, carry):
        for mirrored in range(2):
            (kx, nx), (ky, ny), (kz, nz) = taps_of(v, 0), taps_of(v, 2), taps_of(v, 1)
            if mirrored:
                kx, ky, kz = kx[::-1], ky[::-1], kz[::-1]
            band_z = select(shift_z, kz, 0, 9) * (nx * nz)
            at_v = pl.ds(pl.multiple_of(v * 128, 128), 128)
            for s in range(3):
                block = select(shift_x + 4 * s, kx, max(4 * s - 3, 0), min(4 * s + 4, 9)) * band_z
                if mirrored:
                    flat[s] += jnp.broadcast_to(jnp.sum(block, axis=1, keepdims=True), flat.shape[1:])
                high, low = split(block)
                for part, value in enumerate((high, low, high)):
                    if mirrored:
                        column = pl.ds(pl.multiple_of(v * 384 + part * 128, 128), 128)
                        gather[pl.ds(256 - 128 * s, 128), column] = value
                    else:
                        spread[at_v, pl.ds(384 * s + 128 * part, 128)] = value
            lat = lat_b if mirrored else lat_f
            same = split(select(shift_y, ky, 0, 9) * ny)
            after = split(select(shift_y + 128, ky, 5, 9) * ny)
            before = split(select(shift_y - 128, ky, 0, 4) * ny)
            for part, which in enumerate((0, 1, 0)):
                for b in range(2):
                    for i in range(3):
                        for o in range(2):
                            step = (i + b) - (o + 2 * b)
                            value = {0: same, 1: after, -1: before}.get(step)
                            value = zero if value is None else value[which]
                            lat[v, b, pl.ds(384 * part + 128 * i, 128), pl.ds(128 * o, 128)] = value
        return carry

    flat[...] = jnp.zeros_like(flat)
    lax.fori_loop(0, 4, build, 0)

    ids = cycles[0, :, pl.ds(0, 256)].astype(F32)
    ids = jnp.concatenate([ids, jnp.zeros((128 - depth, 256), F32)], axis=0).T
    bins = lax.broadcasted_iota(jnp.int32, (256, CYCLES), 1).astype(F32)
    for k in range(depth // 2 + 1):
        onehot[pl.ds(256 * k, 256)] = jnp.where(bins == ids[:, k : k + 1], 1.0, 0.0).astype(BF16)

    def put_parts(ref, base, value):
        high, low = split(value)
        ref[pl.ds(base, 128)] = high
        ref[pl.ds(base + 128, 128)] = high
        ref[pl.ds(base + 256, 128)] = low

    def along_y(value, lat, v):
        high, low = split(value)
        for b in range(2):
            at = slice(128 * b, 128 * b + 384)
            lhs = jnp.concatenate([high[:, at], high[:, at], low[:, at]], axis=1)
            yield dot(lhs, lat[v, b])

    def sweep(h):
        put_parts(dext, 0, halo[h, 0])
        put_parts(dext, 384, est[h, pl.ds(0, 128)])
        put_parts(dext, 768, est[h, pl.ds(128, 128)])
        put_parts(dext, 1152, halo[h, 1])
        for i in range(2):
            first[i] = dot(spread[...], dext[pl.ds(384 * i, 1152)])

        for v in range(4):
            at_v = pl.ds(v * 128, 128)
            value = jnp.concatenate([first[0, at_v], first[1, at_v]], axis=0)
            quotient = [
                data[h, v, :, pl.ds(256 * b, 256)].astype(F32) / predicted
                for b, predicted in enumerate(along_y(value, lat_f, v))
            ]
            quotient = jnp.concatenate(quotient, axis=1)
            for b, corrected in enumerate(along_y(quotient, lat_b, v)):
                high, low = split(corrected)
                for part, piece in enumerate((high, high, low)):
                    at = pl.ds(v * 384 + 128 * part, 128)
                    for side in range(2):
                        cs[side, at, pl.ds(256 * b, 256)] = piece[128 * side : 128 * side + 128]

        r0 = dot(gather[...], cs[0])
        corr_mine[h, 0] = r0[:128]
        corr_own[h] = r0[128:]
        r1 = dot(gather[...], cs[1])
        corr_mine[h, 1] = r1[256:]
        corr_own[h] += r1[:256]

    def wide(value):
        return jnp.concatenate([value] * (halo.shape[-1] // 128), axis=1)

    def flat_part(side):
        return wide(flat[0] if side == 0 else flat[2])

    def flat_own(side):
        return wide(flat[1] + (flat[2] if side == 0 else flat[0]))

    def send_both(h):
        for side in range(2):
            both_out[h, side, pl.ds(0, 128)] = (corr_mine[h, side] - flat_part(1 - side)).astype(BF16)
            both_out[h, side, pl.ds(128, 128)] = (
                corr_own[h, pl.ds(128 * side, 128)] - flat_own(side)
            ).astype(BF16)
        start(both_copy, h)

    def send_last(h):
        for side in range(2):
            last_out[h, side] = (corr_mine[h, side] - flat_part(1 - side)).astype(last_out.dtype)
        start(last_copy, h)

    def scale_own(h, side, received):
        at = pl.ds(128 * side, 128)
        near = has_left if side == 0 else has_right
        outside = jnp.where(near, flat_part(side) + received.astype(F32), 0.0)
        est[h, at] = est[h, at] * (0.25 * (corr_own[h, at] + outside))

    def update_both(h):
        wait_send(halo_copy, h)
        wait_recv(both_copy, h)
        for side in range(2):
            scale_own(h, side, both_in[h, side, pl.ds(0, 128)])
            theirs = flat_own(1 - side) + both_in[h, side, pl.ds(128, 128)].astype(F32)
            halo[h, side] = halo[h, side] * (0.25 * (corr_mine[h, side] + theirs))

    def update_last(h):
        wait_recv(last_copy, h)
        for side in range(2):
            scale_own(h, side, last_in[h, side])

    def spectrum(h):
        rows = dot(est[h].astype(BF16), table[...])
        lateral = rows.shape[1] // 2
        for g in range(2):
            at = slice(128 * g, 128 * g + 128)
            both = jnp.concatenate([rows[at, :lateral], rows[at, lateral:]], axis=0)
            high, low = split(both)
            spec[h, g] = dot(forward_z[...], jnp.concatenate([high, high, low], axis=0))

    for h in range(2):
        wait_recv(halo_copy, h)
        sweep(h)
        send_both(h)
    for h in range(2):
        update_both(h)
        sweep(h)
        send_last(h)
    for h in range(2):
        update_last(h)
        spectrum(h)

    lateral = data.shape[3]
    half = depth // 2

    def power(a, b):
        total = jnp.zeros((depth, lateral), F32)
        for g in range(2):
            for at in range(0, 256, depth):
                total = total + spec[a, g, pl.ds(at, depth)] * spec[b, g, pl.ds(at, depth)]
        return total

    lane = lax.broadcasted_iota(jnp.int32, (1, 256), 1)
    weight_l = jnp.where(lane == 0, 1.0, 2.0)
    rows16 = lax.broadcasted_iota(jnp.int32, (half, 256), 0)
    edge = []
    cells = []
    for q, (a, b) in enumerate(((0, 1), (0, 0), (1, 1))):
        total = power(a, b)
        edge.append(jnp.sum(total[:, 256:257], axis=0, keepdims=True))
        low = total[:half, :256]
        high = total[half:, :256]
        pairs = (low + jnp.where(rows16 == 0, 0.0, high)) * weight_l
        last = high[:1] * weight_l
        cells.append([pairs[k : k + 1] for k in range(half)] + [high[:1] * weight_l])

    terms = []
    for k in range(half + 1):
        value = jnp.concatenate([cells[q][k] for q in range(3)] + [jnp.zeros((5, 256), F32)], axis=0)
        a = value.astype(BF16).astype(F32)
        b = (value - a).astype(BF16).astype(F32)
        terms.append(jnp.concatenate([a, b, value - a - b, jnp.zeros_like(a)], axis=0).astype(BF16))
    binned = dot(jnp.concatenate(terms, axis=1), onehot[...])
    binned = binned[0:8] + binned[8:16] + binned[16:24]
    bin_row = lax.broadcasted_iota(jnp.int32, (8, CYCLES), 0)
    bin_lane = lax.broadcasted_iota(jnp.int32, (8, CYCLES), 1)
    for q in range(3):
        binned = binned + jnp.where(
            (bin_row == q) & (bin_lane == CYCLES - 1), jnp.broadcast_to(edge[q], (8, CYCLES)), 0.0
        )
    red_out[...] = binned

    def share(step):
        peer = lax.rem(me + step, n)
        return pltpu.make_async_remote_copy(
            src_ref=red_out,
            dst_ref=red_in.at[step],
            send_sem=red_send.at[step],
            recv_sem=red_recv.at[step],
            device_id={"tile": peer},
            device_id_type=MESH,
        )

    def start_share(step, carry):
        share(step).start()
        return carry

    def wait_share(step, carry):
        share(step).wait()
        return carry + red_in[step]

    lax.fori_loop(1, n, start_share, 0)
    totals = lax.fori_loop(1, n, wait_share, binned)

    corr = totals[0:1] / (jnp.sqrt(totals[1:2]) * jnp.sqrt(totals[2:3]))
    scale = 0.5 / (depth * lateral)
    cycle_weight = jnp.where(lane <= cutoff[0], corr, 0.0) * scale
    low_table = jnp.broadcast_to(cycle_weight[:, :128], (8, 128))
    high_table = jnp.broadcast_to(cycle_weight[:, 128:], (8, 128))
    weights = []
    for r in range(0, half + 8, 8):
        pieces = []
        for c in range(0, lateral, 128):
            ids = cycles[0, pl.ds(r, 8), pl.ds(c, 128)]
            index = ids & 127
            from_low = jnp.take_along_axis(low_table, index, axis=1)
            from_high = jnp.take_along_axis(high_table, index, axis=1)
            pieces.append(jnp.where(ids < 128, from_low, from_high))
        weights.append(jnp.concatenate(pieces, axis=1))
    low = jnp.concatenate(weights[:-1], axis=0)
    row0 = lax.broadcasted_iota(jnp.int32, (half, lateral), 0) == 0
    high = jnp.where(row0, jnp.broadcast_to(weights[-1][0:1], (half, lateral)), low)
    cell = jnp.concatenate([low, high], axis=0)

    for g in range(2):
        mixed = jnp.concatenate(
            [
                (spec[0, g, pl.ds(at, depth)] + spec[1, g, pl.ds(at, depth)]) * cell
                for at in range(0, 256, depth)
            ],
            axis=0,
        )
        high, low = split(mixed)
        inner = dot(inverse_z[...], jnp.concatenate([high, high, low], axis=0)).astype(BF16)
        out[pl.ds(128 * g, 128)] = dot(inner[:128], table[:, pl.ds(0, lateral)]) + dot(
            inner[128:], table[:, pl.ds(lateral, lateral)]
        )

    for h in range(2):
        wait_send(both_copy, h)
        wait_send(last_copy, h)


def body(data_halves, psf_taps, cycle_map, cutoff):
    halves, views, slab, depth, lateral = data_halves.shape
    n = lax.axis_size("tile")
    rows = slab * depth
    table, forward_z, inverse_z = constants(depth, lateral)
    vmem = pl.BlockSpec(memory_space=pltpu.VMEM)
    smem = pl.BlockSpec(memory_space=pltpu.SMEM)
    dma = pltpu.SemaphoreType.DMA
    joined = pl.pallas_call(
        functools.partial(kernel, n),
        out_shape=jax.ShapeDtypeStruct((rows, lateral), F32),
        in_specs=[vmem, smem, vmem, smem, vmem, vmem, vmem],
        out_specs=vmem,
        scratch_shapes=[
            pltpu.VMEM((2, rows, lateral), F32),
            pltpu.VMEM((2, 2, 128, lateral), F32),
            pltpu.VMEM((2, 2, 128, lateral), F32),
            pltpu.VMEM((2, rows, lateral), F32),
            pltpu.VMEM((3, 128, 128), F32),
            pltpu.VMEM((2, 2, 256, lateral), BF16),
            pltpu.VMEM((2, 2, 256, lateral), BF16),
            pltpu.VMEM((2, 2, 128, lateral), BF16),
            pltpu.VMEM((2, 2, 128, lateral), BF16),
            pltpu.VMEM((512, 1152), BF16),
            pltpu.VMEM((384, 1536), BF16),
            pltpu.VMEM((4, 2, 1152, 256), BF16),
            pltpu.VMEM((4, 2, 1152, 256), BF16),
            pltpu.VMEM((1536, lateral), BF16),
            pltpu.VMEM((2, 512, lateral), F32),
            pltpu.VMEM((2, 1536, lateral), BF16),
            pltpu.VMEM(((depth // 2 + 1) * 256, CYCLES), BF16),
            pltpu.VMEM((2, 2, rows, lateral), F32),
            pltpu.VMEM((8, CYCLES), F32),
            pltpu.VMEM((n, 8, CYCLES), F32),
            dma((2, 2)),
            dma((2, 2)),
            dma((2, 2)),
            dma((2, 2)),
            dma((2, 2)),
            dma((2, 2)),
            dma((n,)),
            dma((n,)),
        ],
        compiler_params=pltpu.CompilerParams(
            collective_id=0, has_side_effects=True, vmem_limit_bytes=56 * 1024 * 1024
        ),
    )(
        data_halves.reshape(halves, views, rows, lateral),
        jnp.transpose(psf_taps, (1, 0, 2)),
        cycle_map,
        cutoff,
        jnp.asarray(table),
        jnp.asarray(forward_z),
        jnp.asarray(inverse_z),
    )
    return joined.reshape(slab, depth, lateral)


def solution(mesh):
    in_specs = (
        P(None, None, ("groups", "tile"), None, None),
        P(),
        P(("groups", "tile"), None, None),
        P("groups"),
    )
    out_specs = P(("groups", "tile"), None, None)
    return jax.shard_map(body, mesh=mesh, in_specs=in_specs, out_specs=out_specs, check_vma=False)
```

```python
import functools

import jax
import jax.numpy as jnp
import ml_dtypes
import numpy as np
from jax import lax
from jax.experimental import pallas as pl
from jax.experimental.pallas import tpu as pltpu
from jax.sharding import PartitionSpec as P

CYCLES = 256
MESH = pl.DeviceIdType.MESH
F32 = jnp.float32
BF16 = jnp.bfloat16


def cos_sin(length):
    index_n = np.arange(length)
    phase = index_n[:, None] * index_n[None, :] % length
    angle = phase.astype(np.float32) * np.float32(2.0 * np.pi / length)
    return np.cos(angle).astype(np.float32), np.sin(angle).astype(np.float32)


def split_np(matrix):
    high = matrix.astype(ml_dtypes.bfloat16)
    low = (matrix - high.astype(np.float32)).astype(ml_dtypes.bfloat16)
    return np.concatenate([high, low, high], axis=1)


def constants(depth, lateral):
    half = depth // 2
    order = np.concatenate([np.arange(half + 1), depth - np.arange(1, half)])
    cos_z, sin_z = cos_sin(depth)
    cos_z, sin_z = cos_z[order], sin_z[order]
    eye = np.eye(128 // depth, dtype=np.float32)
    cos_k, sin_k = np.kron(eye, cos_z), np.kron(eye, sin_z)
    forward = np.block([[cos_k, sin_k], [-sin_k, cos_k]])
    inverse = np.ascontiguousarray(forward.T)
    cos_y, sin_y = cos_sin(lateral)
    lateral_table = np.concatenate([cos_y, -sin_y], axis=1).astype(ml_dtypes.bfloat16)
    return lateral_table, split_np(forward), split_np(inverse)


def split(value):
    high = value.astype(BF16)
    low = (value - high.astype(F32)).astype(BF16)
    return high, low


def dot(a, b):
    return lax.dot_general(a, b, (((1,), (0,)), ((), ())), preferred_element_type=F32)


def kernel(
    n, data_far, psf, cycles, cutoff, table_far, forward_far, inverse_far, out,
    data, table, forward_z, inverse_z, near_sem,
    est, halo, corr_mine, corr_own, flat, both_out, both_in, last_out, last_in,
    spread, gather, lat_f, lat_b, dext, first, cs, onehot, spec, red_out, red_in,
    halo_send, halo_recv, both_send, both_recv, last_send, last_recv, red_send, red_recv,
):
    me = lax.axis_index("tile")
    has_left = me > 0
    has_right = me < n - 1

    near = [pltpu.make_async_copy(data_far.at[h], data.at[h], near_sem.at[h]) for h in range(2)]
    near += [
        pltpu.make_async_copy(far, to, near_sem.at[i])
        for i, far, to in ((2, table_far, table), (3, forward_far, forward_z), (4, inverse_far, inverse_z))
    ]
    for copy in near:
        copy.start()

    barrier = pltpu.get_barrier_semaphore()

    def greet(step, carry):
        peer = lax.rem(me + step, n)
        pl.semaphore_signal(barrier, inc=1, device_id={"tile": peer}, device_id_type=MESH)
        return carry

    lax.fori_loop(1, n, greet, 0)

    def neighbour(side):
        return lax.rem(me + n - 1, n) if side == 0 else lax.rem(me + 1, n)

    def halo_copy(h, side):
        return pltpu.make_async_remote_copy(
            src_ref=est.at[h, pl.ds(128 * side, 128)],
            dst_ref=halo.at[h, 1 - side],
            send_sem=halo_send.at[h, side],
            recv_sem=halo_recv.at[h, 1 - side],
            device_id={"tile": neighbour(side)},
            device_id_type=MESH,
        )

    def both_copy(h, side):
        return pltpu.make_async_remote_copy(
            src_ref=both_out.at[h, side],
            dst_ref=both_in.at[h, 1 - side],
            send_sem=both_send.at[h, side],
            recv_sem=both_recv.at[h, 1 - side],
            device_id={"tile": neighbour(side)},
            device_id_type=MESH,
        )

    def last_copy(h, side):
        return pltpu.make_async_remote_copy(
            src_ref=last_out.at[h, side],
            dst_ref=last_in.at[h, 1 - side],
            send_sem=last_send.at[h, side],
            recv_sem=last_recv.at[h, 1 - side],
            device_id={"tile": neighbour(side)},
            device_id_type=MESH,
        )

    def on_side(side, action):
        pl.when(has_left if side == 0 else has_right)(action)

    def start(make, h):
        for side in range(2):
            on_side(side, lambda: make(h, side).start())

    def wait_recv(make, h):
        for side in range(2):
            on_side(side, lambda: make(h, 1 - side).wait_recv())

    def wait_send(make, h):
        for side in range(2):
            on_side(side, lambda: make(h, side).wait_send())

    for h in range(2):
        near[h].wait()
        total = data[h, 0].astype(F32)
        for v in range(1, 4):
            total = total + data[h, v].astype(F32)
        est[h] = total * 0.25
        if h == 0:
            pl.semaphore_wait(barrier, n - 1)
        start(halo_copy, h)

    def clear(side):
        for h in range(2):
            halo[h, side] = jnp.zeros(halo.shape[2:], F32)
            both_in[h, side] = jnp.zeros(both_in.shape[2:], BF16)
            last_in[h, side] = jnp.zeros(last_in.shape[2:], last_in.dtype)

    pl.when(jnp.logical_not(has_left))(lambda: clear(0))
    pl.when(jnp.logical_not(has_right))(lambda: clear(1))

    row = lax.broadcasted_iota(jnp.int32, (128, 128), 0)
    col = lax.broadcasted_iota(jnp.int32, (128, 128), 1)
    depth = data.shape[2] // 8
    shift_y = row - col + 4
    shift_z = col % depth - row % depth + 4
    shift_x = col // depth - row // depth

    def taps_of(v, axis):
        taps = [psf[axis, v, t] for t in range(9)]
        total = taps[0]
        for t in range(1, 9):
            total = total + taps[t]
        return taps, jnp.ones((128, 128), F32) / jnp.full((128, 128), total, F32)

    def select(shift, taps, low, high):
        value = jnp.zeros((128, 128), F32)
        for t in range(low, high):
            value = jnp.where(shift == t, taps[t], value)
        return value

    zero = jnp.zeros((128, 128), BF16)

    def build(v, carry):
        for mirrored in range(2):
            (kx, nx), (ky, ny), (kz, nz) = taps_of(v, 0), taps_of(v, 2), taps_of(v, 1)
            if mirrored:
                kx, ky, kz = kx[::-1], ky[::-1], kz[::-1]
            band_z = select(shift_z, kz, 0, 9) * (nx * nz)
            at_v = pl.ds(pl.multiple_of(v * 128, 128), 128)
            for s in range(3):
                block = select(shift_x + 4 * s, kx, max(4 * s - 3, 0), min(4 * s + 4, 9)) * band_z
                if mirrored:
                    flat[s] += jnp.broadcast_to(jnp.sum(block, axis=1, keepdims=True), flat.shape[1:])
                high, low = split(block)
                for part, value in enumerate((high, low, high)):
                    if mirrored:
                        column = pl.ds(pl.multiple_of(v * 384 + part * 128, 128), 128)
                        gather[pl.ds(256 - 128 * s, 128), column] = value
                    else:
                        spread[at_v, pl.ds(384 * s + 128 * part, 128)] = value
            lat = lat_b if mirrored else lat_f
            same = split(select(shift_y, ky, 0, 9) * ny)
            after = split(select(shift_y + 128, ky, 5, 9) * ny)
            before = split(select(shift_y - 128, ky, 0, 4) * ny)
            for part, which in enumerate((0, 1, 0)):
                for b in range(2):
                    for i in range(3):
                        for o in range(2):
                            step = (i + b) - (o + 2 * b)
                            value = {0: same, 1: after, -1: before}.get(step)
                            value = zero if value is None else value[which]
                            lat[v, b, pl.ds(384 * part + 128 * i, 128), pl.ds(128 * o, 128)] = value
        return carry

    flat[...] = jnp.zeros_like(flat)
    lax.fori_loop(0, 4, build, 0)

    ids = cycles[0, :, pl.ds(0, 256)].astype(F32)
    ids = jnp.concatenate([ids, jnp.zeros((128 - depth, 256), F32)], axis=0).T
    bins = lax.broadcasted_iota(jnp.int32, (256, CYCLES), 1).astype(F32)
    for k in range(depth // 2 + 1):
        onehot[pl.ds(256 * k, 256)] = jnp.where(bins == ids[:, k : k + 1], 1.0, 0.0).astype(BF16)

    def put_parts(ref, base, value):
        high, low = split(value)
        ref[pl.ds(base, 128)] = high
        ref[pl.ds(base + 128, 128)] = high
        ref[pl.ds(base + 256, 128)] = low

    def along_y(value, lat, v):
        high, low = split(value)
        for b in range(2):
            at = slice(128 * b, 128 * b + 384)
            lhs = jnp.concatenate([high[:, at], high[:, at], low[:, at]], axis=1)
            yield dot(lhs, lat[v, b])

    def sweep(h, send):
        put_parts(dext, 0, halo[h, 0])
        put_parts(dext, 384, est[h, pl.ds(0, 128)])
        put_parts(dext, 768, est[h, pl.ds(128, 128)])
        put_parts(dext, 1152, halo[h, 1])
        for i in range(2):
            first[i] = dot(spread[...], dext[pl.ds(384 * i, 1152)])

        def predict(v):
            at_v = pl.ds(v * 128, 128)
            value = jnp.concatenate([first[0, at_v], first[1, at_v]], axis=0)
            return list(along_y(value, lat_f, v))

        def divide(v, predicted):
            quotient = []
            for b in range(2):
                seen = data[h, v, :, pl.ds(256 * b, 256)].astype(F32)
                inverse = pl.reciprocal(predicted[b], approx=True)
                value = seen * inverse
                quotient.append(value + inverse * (seen - predicted[b] * value))
            return jnp.concatenate(quotient, axis=1)

        def spread_back(v, quotient):
            for b, corrected in enumerate(along_y(quotient, lat_b, v)):
                high, low = split(corrected)
                for part, piece in enumerate((high, high, low)):
                    at = pl.ds(v * 384 + 128 * part, 128)
                    for side in range(2):
                        cs[side, at, pl.ds(256 * b, 256)] = piece[128 * side : 128 * side + 128]

        predicted = predict(0)
        for v in range(4):
            following = predict(v + 1) if v < 3 else None
            spread_back(v, divide(v, predicted))
            predicted = following

        send(h)

    def gather_both(h):
        r0 = dot(gather[...], cs[0])
        corr_mine[h, 0] = r0[:128]
        corr_own[h] = r0[128:]
        r1 = dot(gather[...], cs[1])
        corr_mine[h, 1] = r1[256:]
        corr_own[h] += r1[:256]

    def wide(value):
        return jnp.concatenate([value] * (halo.shape[-1] // 128), axis=1)

    def flat_part(side):
        return wide(flat[0] if side == 0 else flat[2])

    def flat_own(side):
        return wide(flat[1] + (flat[2] if side == 0 else flat[0]))

    def send_both(h):
        gather_both(h)
        for side in range(2):
            both_out[h, side, pl.ds(0, 128)] = (corr_mine[h, side] - flat_part(1 - side)).astype(BF16)
            both_out[h, side, pl.ds(128, 128)] = (
                corr_own[h, pl.ds(128 * side, 128)] - flat_own(side)
            ).astype(BF16)
        start(both_copy, h)

    def send_last(h):
        for side in range(2):
            part = dot(gather[pl.ds(256 * side, 128)], cs[side])
            last_out[h, side] = (part - flat_part(1 - side)).astype(last_out.dtype)
        start(last_copy, h)
        corr_own[h] = dot(gather[pl.ds(128, 256)], cs[0])
        corr_own[h] += dot(gather[pl.ds(0, 256)], cs[1])

    def scale_own(h, side, received):
        at = pl.ds(128 * side, 128)
        near = has_left if side == 0 else has_right
        outside = jnp.where(near, flat_part(side) + received.astype(F32), 0.0)
        est[h, at] = est[h, at] * (0.25 * (corr_own[h, at] + outside))

    def update_both(h):
        wait_send(halo_copy, h)
        wait_recv(both_copy, h)
        for side in range(2):
            scale_own(h, side, both_in[h, side, pl.ds(0, 128)])
            theirs = flat_own(1 - side) + both_in[h, side, pl.ds(128, 128)].astype(F32)
            halo[h, side] = halo[h, side] * (0.25 * (corr_mine[h, side] + theirs))

    def update_last(h):
        wait_recv(last_copy, h)
        for side in range(2):
            scale_own(h, side, last_in[h, side])

    def spectrum(h):
        rows = dot(est[h].astype(BF16), table[...])
        lateral = rows.shape[1] // 2
        for g in range(2):
            at = slice(128 * g, 128 * g + 128)
            both = jnp.concatenate([rows[at, :lateral], rows[at, lateral:]], axis=0)
            high, low = split(both)
            spec[h, g] = dot(forward_z[...], jnp.concatenate([high, high, low], axis=0))

    for h in range(2):
        wait_recv(halo_copy, h)
        sweep(h, send_both)
    for h in range(2):
        update_both(h)
        sweep(h, send_last)

    lateral = data.shape[3]
    half = depth // 2

    def power(a, b):
        total = jnp.zeros((depth, lateral), F32)
        for g in range(2):
            for at in range(0, 256, depth):
                total = total + spec[a, g, pl.ds(at, depth)] * spec[b, g, pl.ds(at, depth)]
        return total

    for copy in near[2:]:
        copy.wait()
    update_last(0)
    spectrum(0)
    power_0 = power(0, 0)
    update_last(1)
    spectrum(1)
    powers = (power(0, 1), power_0, power(1, 1))

    lane = lax.broadcasted_iota(jnp.int32, (1, 256), 1)
    weight_l = jnp.where(lane == 0, 1.0, 2.0)
    rows16 = lax.broadcasted_iota(jnp.int32, (half, 256), 0)
    edge = []
    cells = []
    for q, total in enumerate(powers):
        edge.append(jnp.sum(total[:, 256:257], axis=0, keepdims=True))
        low = total[:half, :256]
        high = total[half:, :256]
        pairs = (low + jnp.where(rows16 == 0, 0.0, high)) * weight_l
        last = high[:1] * weight_l
        cells.append([pairs[k : k + 1] for k in range(half)] + [high[:1] * weight_l])

    terms = []
    for k in range(half + 1):
        value = jnp.concatenate([cells[q][k] for q in range(3)] + [jnp.zeros((5, 256), F32)], axis=0)
        a = value.astype(BF16).astype(F32)
        b = (value - a).astype(BF16).astype(F32)
        terms.append(jnp.concatenate([a, b, value - a - b, jnp.zeros_like(a)], axis=0).astype(BF16))
    binned = dot(jnp.concatenate(terms, axis=1), onehot[...])
    binned = binned[0:8] + binned[8:16] + binned[16:24]
    bin_row = lax.broadcasted_iota(jnp.int32, (8, CYCLES), 0)
    bin_lane = lax.broadcasted_iota(jnp.int32, (8, CYCLES), 1)
    for q in range(3):
        binned = binned + jnp.where(
            (bin_row == q) & (bin_lane == CYCLES - 1), jnp.broadcast_to(edge[q], (8, CYCLES)), 0.0
        )
    red_out[...] = binned

    def share(step):
        peer = lax.rem(me + step, n)
        return pltpu.make_async_remote_copy(
            src_ref=red_out,
            dst_ref=red_in.at[step],
            send_sem=red_send.at[step],
            recv_sem=red_recv.at[step],
            device_id={"tile": peer},
            device_id_type=MESH,
        )

    def start_share(step, carry):
        share(step).start()
        return carry

    def wait_share(step, carry):
        share(step).wait()
        return carry + red_in[step]

    lax.fori_loop(1, n, start_share, 0)
    totals = lax.fori_loop(1, n, wait_share, binned)

    corr = totals[0:1] / (jnp.sqrt(totals[1:2]) * jnp.sqrt(totals[2:3]))
    scale = 0.5 / (depth * lateral)
    cycle_weight = jnp.where(lane <= cutoff[0], corr, 0.0) * scale
    low_table = jnp.broadcast_to(cycle_weight[:, :128], (8, 128))
    high_table = jnp.broadcast_to(cycle_weight[:, 128:], (8, 128))
    weights = []
    for r in range(0, half + 8, 8):
        pieces = []
        for c in range(0, lateral, 128):
            ids = cycles[0, pl.ds(r, 8), pl.ds(c, 128)]
            index = ids & 127
            from_low = jnp.take_along_axis(low_table, index, axis=1)
            from_high = jnp.take_along_axis(high_table, index, axis=1)
            pieces.append(jnp.where(ids < 128, from_low, from_high))
        weights.append(jnp.concatenate(pieces, axis=1))
    low = jnp.concatenate(weights[:-1], axis=0)
    row0 = lax.broadcasted_iota(jnp.int32, (half, lateral), 0) == 0
    high = jnp.where(row0, jnp.broadcast_to(weights[-1][0:1], (half, lateral)), low)
    cell = jnp.concatenate([low, high], axis=0)

    for g in range(2):
        mixed = jnp.concatenate(
            [
                (spec[0, g, pl.ds(at, depth)] + spec[1, g, pl.ds(at, depth)]) * cell
                for at in range(0, 256, depth)
            ],
            axis=0,
        )
        high, low = split(mixed)
        inner = dot(inverse_z[...], jnp.concatenate([high, high, low], axis=0)).astype(BF16)
        out[pl.ds(128 * g, 128)] = dot(inner[:128], table[:, pl.ds(0, lateral)]) + dot(
            inner[128:], table[:, pl.ds(lateral, lateral)]
        )

    for h in range(2):
        wait_send(both_copy, h)
        wait_send(last_copy, h)


def body(data_halves, psf_taps, cycle_map, cutoff):
    halves, views, slab, depth, lateral = data_halves.shape
    n = lax.axis_size("tile")
    rows = slab * depth
    table, forward_z, inverse_z = constants(depth, lateral)
    vmem = pl.BlockSpec(memory_space=pltpu.VMEM)
    smem = pl.BlockSpec(memory_space=pltpu.SMEM)
    far = pl.BlockSpec(memory_space=pl.ANY)
    dma = pltpu.SemaphoreType.DMA
    joined = pl.pallas_call(
        functools.partial(kernel, n),
        out_shape=jax.ShapeDtypeStruct((rows, lateral), F32),
        in_specs=[far, smem, vmem, smem, far, far, far],
        out_specs=vmem,
        scratch_shapes=[
            pltpu.VMEM((halves, views, rows, lateral), BF16),
            pltpu.VMEM(table.shape, BF16),
            pltpu.VMEM(forward_z.shape, BF16),
            pltpu.VMEM(inverse_z.shape, BF16),
            dma((5,)),
            pltpu.VMEM((2, rows, lateral), F32),
            pltpu.VMEM((2, 2, 128, lateral), F32),
            pltpu.VMEM((2, 2, 128, lateral), F32),
            pltpu.VMEM((2, rows, lateral), F32),
            pltpu.VMEM((3, 128, 128), F32),
            pltpu.VMEM((2, 2, 256, lateral), BF16),
            pltpu.VMEM((2, 2, 256, lateral), BF16),
            pltpu.VMEM((2, 2, 128, lateral), BF16),
            pltpu.VMEM((2, 2, 128, lateral), BF16),
            pltpu.VMEM((512, 1152), BF16),
            pltpu.VMEM((384, 1536), BF16),
            pltpu.VMEM((4, 2, 1152, 256), BF16),
            pltpu.VMEM((4, 2, 1152, 256), BF16),
            pltpu.VMEM((1536, lateral), BF16),
            pltpu.VMEM((2, 512, lateral), F32),
            pltpu.VMEM((2, 1536, lateral), BF16),
            pltpu.VMEM(((depth // 2 + 1) * 256, CYCLES), BF16),
            pltpu.VMEM((2, 2, rows, lateral), F32),
            pltpu.VMEM((8, CYCLES), F32),
            pltpu.VMEM((n, 8, CYCLES), F32),
            dma((2, 2)),
            dma((2, 2)),
            dma((2, 2)),
            dma((2, 2)),
            dma((2, 2)),
            dma((2, 2)),
            dma((n,)),
            dma((n,)),
        ],
        compiler_params=pltpu.CompilerParams(
            collective_id=0, has_side_effects=True, vmem_limit_bytes=56 * 1024 * 1024
        ),
    )(
        data_halves.reshape(halves, views, rows, lateral),
        jnp.transpose(psf_taps, (1, 0, 2)),
        cycle_map,
        cutoff,
        jnp.asarray(table),
        jnp.asarray(forward_z),
        jnp.asarray(inverse_z),
    )
    return joined.reshape(slab, depth, lateral)


def solution(mesh):
    in_specs = (
        P(None, None, ("groups", "tile"), None, None),
        P(),
        P(("groups", "tile"), None, None),
        P("groups"),
    )
    out_specs = P(("groups", "tile"), None, None)
    return jax.shard_map(body, mesh=mesh, in_specs=in_specs, out_specs=out_specs, check_vma=False)
```

```python
import functools

import jax
import jax.numpy as jnp
import ml_dtypes
import numpy as np
from jax import lax
from jax.experimental import pallas as pl
from jax.experimental.pallas import tpu as pltpu
from jax.sharding import PartitionSpec as P

CYCLES = 256
MESH = pl.DeviceIdType.MESH
F32 = jnp.float32
BF16 = jnp.bfloat16


def cos_sin(length):
    index_n = np.arange(length)
    phase = index_n[:, None] * index_n[None, :] % length
    angle = phase.astype(np.float32) * np.float32(2.0 * np.pi / length)
    return np.cos(angle).astype(np.float32), np.sin(angle).astype(np.float32)


def split_np(matrix):
    high = matrix.astype(ml_dtypes.bfloat16)
    low = (matrix - high.astype(np.float32)).astype(ml_dtypes.bfloat16)
    return np.concatenate([high, low, high], axis=1)


def constants(depth, lateral):
    half = depth // 2
    order = np.concatenate([np.arange(half + 1), depth - np.arange(1, half)])
    cos_z, sin_z = cos_sin(depth)
    cos_z, sin_z = cos_z[order], sin_z[order]
    eye = np.eye(128 // depth, dtype=np.float32)
    cos_k, sin_k = np.kron(eye, cos_z), np.kron(eye, sin_z)
    forward = np.block([[cos_k, sin_k], [-sin_k, cos_k]])
    inverse = np.ascontiguousarray(forward.T)
    cos_y, sin_y = cos_sin(lateral)
    lateral_table = np.concatenate([cos_y, -sin_y], axis=1).astype(ml_dtypes.bfloat16)
    return lateral_table, split_np(forward), split_np(inverse)


def split(value):
    high = value.astype(BF16)
    low = (value - high.astype(F32)).astype(BF16)
    return high, low


def dot(a, b):
    return lax.dot_general(a, b, (((1,), (0,)), ((), ())), preferred_element_type=F32)


def kernel(
    n, data_far, psf, cycles, cutoff, table_far, forward_far, inverse_far, out,
    data, table, forward_z, inverse_z, near_sem,
    est, halo, corr_mine, corr_own, flat, both_out, both_in, last_out, last_in,
    spread, gather, lat_f, lat_b, dext, first, cs, onehot, spec, red_out, red_in,
    halo_send, halo_recv, both_send, both_recv, last_send, last_recv, red_send, red_recv,
):
    me = lax.axis_index("tile")
    has_left = me > 0
    has_right = me < n - 1

    near = [pltpu.make_async_copy(data_far.at[h], data.at[h], near_sem.at[h]) for h in range(2)]
    near += [
        pltpu.make_async_copy(far, to, near_sem.at[i])
        for i, far, to in ((2, table_far, table), (3, forward_far, forward_z), (4, inverse_far, inverse_z))
    ]
    for copy in near:
        copy.start()

    barrier = pltpu.get_barrier_semaphore()

    def greet(step, carry):
        peer = lax.rem(me + step, n)
        pl.semaphore_signal(barrier, inc=1, device_id={"tile": peer}, device_id_type=MESH)
        return carry

    lax.fori_loop(1, n, greet, 0)

    def neighbour(side):
        return lax.rem(me + n - 1, n) if side == 0 else lax.rem(me + 1, n)

    def halo_copy(h, side):
        return pltpu.make_async_remote_copy(
            src_ref=est.at[h, pl.ds(128 * side, 128)],
            dst_ref=halo.at[h, 1 - side],
            send_sem=halo_send.at[h, side],
            recv_sem=halo_recv.at[h, 1 - side],
            device_id={"tile": neighbour(side)},
            device_id_type=MESH,
        )

    def both_copy(h, side):
        return pltpu.make_async_remote_copy(
            src_ref=both_out.at[h, side],
            dst_ref=both_in.at[h, 1 - side],
            send_sem=both_send.at[h, side],
            recv_sem=both_recv.at[h, 1 - side],
            device_id={"tile": neighbour(side)},
            device_id_type=MESH,
        )

    def last_copy(h, side):
        return pltpu.make_async_remote_copy(
            src_ref=last_out.at[h, side],
            dst_ref=last_in.at[h, 1 - side],
            send_sem=last_send.at[h, side],
            recv_sem=last_recv.at[h, 1 - side],
            device_id={"tile": neighbour(side)},
            device_id_type=MESH,
        )

    def on_side(side, action):
        pl.when(has_left if side == 0 else has_right)(action)

    def start(make, h):
        for side in range(2):
            on_side(side, lambda: make(h, side).start())

    def wait_recv(make, h):
        for side in range(2):
            on_side(side, lambda: make(h, 1 - side).wait_recv())

    def wait_send(make, h):
        for side in range(2):
            on_side(side, lambda: make(h, side).wait_send())

    for h in range(2):
        near[h].wait()
        total = data[h, 0].astype(F32)
        for v in range(1, 4):
            total = total + data[h, v].astype(F32)
        est[h] = total * 0.25
        if h == 0:
            pl.semaphore_wait(barrier, n - 1)
        start(halo_copy, h)

    def clear(side):
        for h in range(2):
            halo[h, side] = jnp.zeros(halo.shape[2:], F32)
            both_in[h, side] = jnp.zeros(both_in.shape[2:], BF16)
            last_in[h, side] = jnp.zeros(last_in.shape[2:], last_in.dtype)

    pl.when(jnp.logical_not(has_left))(lambda: clear(0))
    pl.when(jnp.logical_not(has_right))(lambda: clear(1))

    row = lax.broadcasted_iota(jnp.int32, (128, 128), 0)
    col = lax.broadcasted_iota(jnp.int32, (128, 128), 1)
    depth = data.shape[2] // 8
    shift_y = row - col + 4
    shift_z = col % depth - row % depth + 4
    shift_x = col // depth - row // depth

    def taps_of(v, axis):
        taps = [psf[axis, v, t] for t in range(9)]
        total = taps[0]
        for t in range(1, 9):
            total = total + taps[t]
        return taps, jnp.ones((128, 128), F32) / jnp.full((128, 128), total, F32)

    def select(shift, taps, low, high):
        value = jnp.zeros((128, 128), F32)
        for t in range(low, high):
            value = jnp.where(shift == t, taps[t], value)
        return value

    zero = jnp.zeros((128, 128), BF16)

    def build(v, carry):
        for mirrored in range(2):
            (kx, nx), (ky, ny), (kz, nz) = taps_of(v, 0), taps_of(v, 2), taps_of(v, 1)
            if mirrored:
                kx, ky, kz = kx[::-1], ky[::-1], kz[::-1]
            band_z = select(shift_z, kz, 0, 9) * (nx * nz)
            at_v = pl.ds(pl.multiple_of(v * 128, 128), 128)
            for s in range(3):
                block = select(shift_x + 4 * s, kx, max(4 * s - 3, 0), min(4 * s + 4, 9)) * band_z
                if mirrored:
                    flat[s] += jnp.broadcast_to(jnp.sum(block, axis=1, keepdims=True), flat.shape[1:])
                high, low = split(block)
                for part, value in enumerate((high, low, high)):
                    if mirrored:
                        column = pl.ds(pl.multiple_of(v * 384 + part * 128, 128), 128)
                        gather[pl.ds(256 - 128 * s, 128), column] = value
                    else:
                        spread[at_v, pl.ds(384 * s + 128 * part, 128)] = value
            lat = lat_b if mirrored else lat_f
            same = split(select(shift_y, ky, 0, 9) * ny)
            after = split(select(shift_y + 128, ky, 5, 9) * ny)
            before = split(select(shift_y - 128, ky, 0, 4) * ny)
            for part, which in enumerate((0, 1, 0)):
                for i in range(2):
                    for o in range(2):
                        at = pl.ds(256 * part + 128 * i, 128), pl.ds(128 * o, 128)
                        value = (same, after, before)[i - o][which]
                        lat[(v, 0) + at] = value
                        lat[(v, 1) + at] = zero if i == o else value
        return carry

    flat[...] = jnp.zeros_like(flat)
    lax.fori_loop(0, 4, build, 0)

    ids = cycles[0, :, pl.ds(0, 256)].astype(F32)
    ids = jnp.concatenate([ids, jnp.zeros((128 - depth, 256), F32)], axis=0).T
    bins = lax.broadcasted_iota(jnp.int32, (256, CYCLES), 1).astype(F32)
    for k in range(depth // 2 + 1):
        onehot[pl.ds(256 * k, 256)] = jnp.where(bins == ids[:, k : k + 1], 1.0, 0.0).astype(BF16)

    def put_parts(ref, base, value):
        high, low = split(value)
        ref[pl.ds(base, 128)] = high
        ref[pl.ds(base + 128, 128)] = high
        ref[pl.ds(base + 256, 128)] = low

    def three(high, low, at):
        return jnp.concatenate([high[:, at], high[:, at], low[:, at]], axis=1)

    def along_y(value, lat, v):
        high, low = split(value)
        halves = [three(high, low, slice(0, 256)), three(high, low, slice(256, 512))]
        inside = dot(jnp.concatenate(halves, axis=0), lat[v, 0])
        across = dot(three(high, low, slice(128, 384)), lat[v, 1])
        rows = value.shape[0]
        yield jnp.concatenate([inside[:rows, :128], inside[:rows, 128:] + across[:, :128]], axis=1)
        yield jnp.concatenate([inside[rows:, :128] + across[:, 128:], inside[rows:, 128:]], axis=1)

    def sweep(h, send):
        put_parts(dext, 0, halo[h, 0])
        put_parts(dext, 384, est[h, pl.ds(0, 128)])
        put_parts(dext, 768, est[h, pl.ds(128, 128)])
        put_parts(dext, 1152, halo[h, 1])
        for i in range(2):
            first[i] = dot(spread[...], dext[pl.ds(384 * i, 1152)])

        def predict(v):
            at_v = pl.ds(v * 128, 128)
            value = jnp.concatenate([first[0, at_v], first[1, at_v]], axis=0)
            return list(along_y(value, lat_f, v))

        def divide(v, predicted):
            quotient = []
            for b in range(2):
                seen = data[h, v, :, pl.ds(256 * b, 256)].astype(F32)
                inverse = pl.reciprocal(predicted[b], approx=True)
                value = seen * inverse
                quotient.append(value + inverse * (seen - predicted[b] * value))
            return jnp.concatenate(quotient, axis=1)

        def spread_back(v, quotient):
            for b, corrected in enumerate(along_y(quotient, lat_b, v)):
                high, low = split(corrected)
                for part, piece in enumerate((high, high, low)):
                    at = pl.ds(v * 384 + 128 * part, 128)
                    for side in range(2):
                        cs[side, at, pl.ds(256 * b, 256)] = piece[128 * side : 128 * side + 128]

        predicted = predict(0)
        for v in range(4):
            following = predict(v + 1) if v < 3 else None
            spread_back(v, divide(v, predicted))
            predicted = following

        send(h)

    def gather_both(h):
        r0 = dot(gather[...], cs[0])
        corr_mine[h, 0] = r0[:128]
        corr_own[h] = r0[128:]
        r1 = dot(gather[...], cs[1])
        corr_mine[h, 1] = r1[256:]
        corr_own[h] += r1[:256]

    def wide(value):
        return jnp.concatenate([value] * (halo.shape[-1] // 128), axis=1)

    def flat_part(side):
        return wide(flat[0] if side == 0 else flat[2])

    def flat_own(side):
        return wide(flat[1] + (flat[2] if side == 0 else flat[0]))

    def send_both(h):
        gather_both(h)
        for side in range(2):
            both_out[h, side, pl.ds(0, 128)] = (corr_mine[h, side] - flat_part(1 - side)).astype(BF16)
            both_out[h, side, pl.ds(128, 128)] = (
                corr_own[h, pl.ds(128 * side, 128)] - flat_own(side)
            ).astype(BF16)
        start(both_copy, h)

    def send_last(h):
        for side in range(2):
            part = dot(gather[pl.ds(256 * side, 128)], cs[side])
            last_out[h, side] = (part - flat_part(1 - side)).astype(last_out.dtype)
        start(last_copy, h)
        corr_own[h] = dot(gather[pl.ds(128, 256)], cs[0])
        corr_own[h] += dot(gather[pl.ds(0, 256)], cs[1])

    def scale_own(h, side, received):
        at = pl.ds(128 * side, 128)
        near = has_left if side == 0 else has_right
        outside = jnp.where(near, flat_part(side) + received.astype(F32), 0.0)
        est[h, at] = est[h, at] * (0.25 * (corr_own[h, at] + outside))

    def update_both(h):
        wait_send(halo_copy, h)
        wait_recv(both_copy, h)
        for side in range(2):
            scale_own(h, side, both_in[h, side, pl.ds(0, 128)])
            theirs = flat_own(1 - side) + both_in[h, side, pl.ds(128, 128)].astype(F32)
            halo[h, side] = halo[h, side] * (0.25 * (corr_mine[h, side] + theirs))

    def update_last(h):
        wait_recv(last_copy, h)
        for side in range(2):
            scale_own(h, side, last_in[h, side])

    def spectrum(h):
        rows = dot(est[h].astype(BF16), table[...])
        lateral = rows.shape[1] // 2
        for g in range(2):
            at = slice(128 * g, 128 * g + 128)
            both = jnp.concatenate([rows[at, :lateral], rows[at, lateral:]], axis=0)
            high, low = split(both)
            spec[h, g] = dot(forward_z[...], jnp.concatenate([high, high, low], axis=0))

    for h in range(2):
        wait_recv(halo_copy, h)
        sweep(h, send_both)
    for h in range(2):
        update_both(h)
        sweep(h, send_last)

    lateral = data.shape[3]
    half = depth // 2

    def power(a, b):
        total = jnp.zeros((depth, lateral), F32)
        for g in range(2):
            for at in range(0, 256, depth):
                total = total + spec[a, g, pl.ds(at, depth)] * spec[b, g, pl.ds(at, depth)]
        return total

    for copy in near[2:]:
        copy.wait()
    update_last(0)
    spectrum(0)
    power_0 = power(0, 0)
    update_last(1)
    spectrum(1)
    powers = (power(0, 1), power_0, power(1, 1))

    lane = lax.broadcasted_iota(jnp.int32, (1, 256), 1)
    weight_l = jnp.where(lane == 0, 1.0, 2.0)
    rows16 = lax.broadcasted_iota(jnp.int32, (half, 256), 0)
    edge = []
    cells = []
    for q, total in enumerate(powers):
        edge.append(jnp.sum(total[:, 256:257], axis=0, keepdims=True))
        low = total[:half, :256]
        high = total[half:, :256]
        pairs = (low + jnp.where(rows16 == 0, 0.0, high)) * weight_l
        last = high[:1] * weight_l
        cells.append([pairs[k : k + 1] for k in range(half)] + [high[:1] * weight_l])

    terms = []
    for k in range(half + 1):
        value = jnp.concatenate([cells[q][k] for q in range(3)] + [jnp.zeros((5, 256), F32)], axis=0)
        a = value.astype(BF16).astype(F32)
        b = (value - a).astype(BF16).astype(F32)
        terms.append(jnp.concatenate([a, b, value - a - b, jnp.zeros_like(a)], axis=0).astype(BF16))
    binned = dot(jnp.concatenate(terms, axis=1), onehot[...])
    binned = binned[0:8] + binned[8:16] + binned[16:24]
    bin_row = lax.broadcasted_iota(jnp.int32, (8, CYCLES), 0)
    bin_lane = lax.broadcasted_iota(jnp.int32, (8, CYCLES), 1)
    for q in range(3):
        binned = binned + jnp.where(
            (bin_row == q) & (bin_lane == CYCLES - 1), jnp.broadcast_to(edge[q], (8, CYCLES)), 0.0
        )
    red_out[...] = binned

    def share(step):
        peer = lax.rem(me + step, n)
        return pltpu.make_async_remote_copy(
            src_ref=red_out,
            dst_ref=red_in.at[step],
            send_sem=red_send.at[step],
            recv_sem=red_recv.at[step],
            device_id={"tile": peer},
            device_id_type=MESH,
        )

    def start_share(step, carry):
        share(step).start()
        return carry

    def wait_share(step, carry):
        share(step).wait()
        return carry + red_in[step]

    lax.fori_loop(1, n, start_share, 0)
    totals = lax.fori_loop(1, n, wait_share, binned)

    corr = totals[0:1] / (jnp.sqrt(totals[1:2]) * jnp.sqrt(totals[2:3]))
    scale = 0.5 / (depth * lateral)
    cycle_weight = jnp.where(lane <= cutoff[0], corr, 0.0) * scale
    low_table = jnp.broadcast_to(cycle_weight[:, :128], (8, 128))
    high_table = jnp.broadcast_to(cycle_weight[:, 128:], (8, 128))
    weights = []
    for r in range(0, half + 8, 8):
        pieces = []
        for c in range(0, lateral, 128):
            ids = cycles[0, pl.ds(r, 8), pl.ds(c, 128)]
            index = ids & 127
            from_low = jnp.take_along_axis(low_table, index, axis=1)
            from_high = jnp.take_along_axis(high_table, index, axis=1)
            pieces.append(jnp.where(ids < 128, from_low, from_high))
        weights.append(jnp.concatenate(pieces, axis=1))
    low = jnp.concatenate(weights[:-1], axis=0)
    row0 = lax.broadcasted_iota(jnp.int32, (half, lateral), 0) == 0
    high = jnp.where(row0, jnp.broadcast_to(weights[-1][0:1], (half, lateral)), low)
    cell = jnp.concatenate([low, high], axis=0)

    for g in range(2):
        mixed = jnp.concatenate(
            [
                (spec[0, g, pl.ds(at, depth)] + spec[1, g, pl.ds(at, depth)]) * cell
                for at in range(0, 256, depth)
            ],
            axis=0,
        )
        high, low = split(mixed)
        inner = dot(inverse_z[...], jnp.concatenate([high, high, low], axis=0)).astype(BF16)
        out[pl.ds(128 * g, 128)] = dot(inner[:128], table[:, pl.ds(0, lateral)]) + dot(
            inner[128:], table[:, pl.ds(lateral, lateral)]
        )

    for h in range(2):
        wait_send(both_copy, h)
        wait_send(last_copy, h)


def body(data_halves, psf_taps, cycle_map, cutoff):
    halves, views, slab, depth, lateral = data_halves.shape
    n = lax.axis_size("tile")
    rows = slab * depth
    table, forward_z, inverse_z = constants(depth, lateral)
    vmem = pl.BlockSpec(memory_space=pltpu.VMEM)
    smem = pl.BlockSpec(memory_space=pltpu.SMEM)
    far = pl.BlockSpec(memory_space=pl.ANY)
    dma = pltpu.SemaphoreType.DMA
    joined = pl.pallas_call(
        functools.partial(kernel, n),
        out_shape=jax.ShapeDtypeStruct((rows, lateral), F32),
        in_specs=[far, smem, vmem, smem, far, far, far],
        out_specs=vmem,
        scratch_shapes=[
            pltpu.VMEM((halves, views, rows, lateral), BF16),
            pltpu.VMEM(table.shape, BF16),
            pltpu.VMEM(forward_z.shape, BF16),
            pltpu.VMEM(inverse_z.shape, BF16),
            dma((5,)),
            pltpu.VMEM((2, rows, lateral), F32),
            pltpu.VMEM((2, 2, 128, lateral), F32),
            pltpu.VMEM((2, 2, 128, lateral), F32),
            pltpu.VMEM((2, rows, lateral), F32),
            pltpu.VMEM((3, 128, 128), F32),
            pltpu.VMEM((2, 2, 256, lateral), BF16),
            pltpu.VMEM((2, 2, 256, lateral), BF16),
            pltpu.VMEM((2, 2, 128, lateral), BF16),
            pltpu.VMEM((2, 2, 128, lateral), BF16),
            pltpu.VMEM((512, 1152), BF16),
            pltpu.VMEM((384, 1536), BF16),
            pltpu.VMEM((4, 2, 768, 256), BF16),
            pltpu.VMEM((4, 2, 768, 256), BF16),
            pltpu.VMEM((1536, lateral), BF16),
            pltpu.VMEM((2, 512, lateral), F32),
            pltpu.VMEM((2, 1536, lateral), BF16),
            pltpu.VMEM(((depth // 2 + 1) * 256, CYCLES), BF16),
            pltpu.VMEM((2, 2, rows, lateral), F32),
            pltpu.VMEM((8, CYCLES), F32),
            pltpu.VMEM((n, 8, CYCLES), F32),
            dma((2, 2)),
            dma((2, 2)),
            dma((2, 2)),
            dma((2, 2)),
            dma((2, 2)),
            dma((2, 2)),
            dma((n,)),
            dma((n,)),
        ],
        compiler_params=pltpu.CompilerParams(
            collective_id=0, has_side_effects=True, vmem_limit_bytes=56 * 1024 * 1024
        ),
    )(
        data_halves.reshape(halves, views, rows, lateral),
        jnp.transpose(psf_taps, (1, 0, 2)),
        cycle_map,
        cutoff,
        jnp.asarray(table),
        jnp.asarray(forward_z),
        jnp.asarray(inverse_z),
    )
    return joined.reshape(slab, depth, lateral)


def solution(mesh):
    in_specs = (
        P(None, None, ("groups", "tile"), None, None),
        P(),
        P(("groups", "tile"), None, None),
        P("groups"),
    )
    out_specs = P(("groups", "tile"), None, None)
    return jax.shard_map(body, mesh=mesh, in_specs=in_specs, out_specs=out_specs, check_vma=False)
```

```python
import functools

import jax
import jax.numpy as jnp
import ml_dtypes
import numpy as np
from jax import lax
from jax.experimental import pallas as pl
from jax.experimental.pallas import tpu as pltpu
from jax.sharding import PartitionSpec as P

CYCLES = 256
MESH = pl.DeviceIdType.MESH
F32 = jnp.float32
BF16 = jnp.bfloat16


def cos_sin(length):
    index_n = np.arange(length)
    phase = index_n[:, None] * index_n[None, :] % length
    angle = phase.astype(np.float32) * np.float32(2.0 * np.pi / length)
    return np.cos(angle).astype(np.float32), np.sin(angle).astype(np.float32)


def split_np(matrix):
    high = matrix.astype(ml_dtypes.bfloat16)
    low = (matrix - high.astype(np.float32)).astype(ml_dtypes.bfloat16)
    return np.concatenate([high, low, high], axis=1)


def constants(depth, lateral):
    half = depth // 2
    order = np.concatenate([np.arange(half + 1), depth - np.arange(1, half)])
    cos_z, sin_z = cos_sin(depth)
    cos_z, sin_z = cos_z[order], sin_z[order]
    eye = np.eye(128 // depth, dtype=np.float32)
    cos_k, sin_k = np.kron(eye, cos_z), np.kron(eye, sin_z)
    forward = np.block([[cos_k, sin_k], [-sin_k, cos_k]])
    inverse = np.ascontiguousarray(forward.T)
    cos_y, sin_y = cos_sin(lateral)
    lateral_table = np.concatenate([cos_y, -sin_y], axis=1).astype(ml_dtypes.bfloat16)
    return lateral_table, split_np(forward), split_np(inverse)


def split(value):
    high = value.astype(BF16)
    low = (value - high.astype(F32)).astype(BF16)
    return high, low


def dot(a, b):
    return lax.dot_general(a, b, (((1,), (0,)), ((), ())), preferred_element_type=F32)


def kernel(
    n, data_far, psf, cycles, cutoff, table_far, forward_far, inverse_far, out,
    data, table, forward_z, inverse_z, near_sem,
    est, halo, corr_mine, corr_own, flat, both_out, both_in, last_out, last_in,
    spread, gather, lat_f, lat_b, dext, first, cs, onehot, spec, red_out, red_in,
    halo_send, halo_recv, both_send, both_recv, last_send, last_recv, red_send, red_recv,
):
    me = lax.axis_index("tile")
    has_left = me > 0
    has_right = me < n - 1

    near = [pltpu.make_async_copy(data_far.at[h], data.at[h], near_sem.at[h]) for h in range(2)]
    near += [
        pltpu.make_async_copy(far, to, near_sem.at[i])
        for i, far, to in ((2, table_far, table), (3, forward_far, forward_z), (4, inverse_far, inverse_z))
    ]
    for copy in near:
        copy.start()

    barrier = pltpu.get_barrier_semaphore()

    def greet(step, carry):
        peer = lax.rem(me + step, n)
        pl.semaphore_signal(barrier, inc=1, device_id={"tile": peer}, device_id_type=MESH)
        return carry

    lax.fori_loop(1, n, greet, 0)

    def neighbour(side):
        return lax.rem(me + n - 1, n) if side == 0 else lax.rem(me + 1, n)

    def halo_copy(h, side):
        return pltpu.make_async_remote_copy(
            src_ref=est.at[h, pl.ds(128 * side, 128)],
            dst_ref=halo.at[h, 1 - side],
            send_sem=halo_send.at[h, side],
            recv_sem=halo_recv.at[h, 1 - side],
            device_id={"tile": neighbour(side)},
            device_id_type=MESH,
        )

    def both_copy(h, side):
        return pltpu.make_async_remote_copy(
            src_ref=both_out.at[h, side],
            dst_ref=both_in.at[h, 1 - side],
            send_sem=both_send.at[h, side],
            recv_sem=both_recv.at[h, 1 - side],
            device_id={"tile": neighbour(side)},
            device_id_type=MESH,
        )

    def last_copy(h, side):
        return pltpu.make_async_remote_copy(
            src_ref=last_out.at[h, side],
            dst_ref=last_in.at[h, 1 - side],
            send_sem=last_send.at[h, side],
            recv_sem=last_recv.at[h, 1 - side],
            device_id={"tile": neighbour(side)},
            device_id_type=MESH,
        )

    def on_side(side, action):
        pl.when(has_left if side == 0 else has_right)(action)

    def start(make, h):
        for side in range(2):
            on_side(side, lambda: make(h, side).start())

    def wait_recv(make, h):
        for side in range(2):
            on_side(side, lambda: make(h, 1 - side).wait_recv())

    def wait_send(make, h):
        for side in range(2):
            on_side(side, lambda: make(h, side).wait_send())

    for h in range(2):
        near[h].wait()
        total = data[h, 0].astype(F32)
        for v in range(1, 4):
            total = total + data[h, v].astype(F32)
        est[h] = total * 0.25
        if h == 0:
            pl.semaphore_wait(barrier, n - 1)
        start(halo_copy, h)

    def clear(side):
        for h in range(2):
            halo[h, side] = jnp.zeros(halo.shape[2:], F32)
            both_in[h, side] = jnp.zeros(both_in.shape[2:], BF16)
            last_in[h, side] = jnp.zeros(last_in.shape[2:], last_in.dtype)

    pl.when(jnp.logical_not(has_left))(lambda: clear(0))
    pl.when(jnp.logical_not(has_right))(lambda: clear(1))

    row = lax.broadcasted_iota(jnp.int32, (128, 128), 0)
    col = lax.broadcasted_iota(jnp.int32, (128, 128), 1)
    depth = data.shape[2] // 8
    shift_y = row - col + 4
    shift_z = col % depth - row % depth + 4
    shift_x = col // depth - row // depth

    def taps_of(v, axis):
        taps = [psf[axis, v, t] for t in range(9)]
        total = taps[0]
        for t in range(1, 9):
            total = total + taps[t]
        return taps, jnp.ones((128, 128), F32) / jnp.full((128, 128), total, F32)

    def select(shift, taps, low, high):
        value = jnp.zeros((128, 128), F32)
        for t in range(low, high):
            value = jnp.where(shift == t, taps[t], value)
        return value

    zero = jnp.zeros((128, 128), BF16)

    def build(v, carry):
        for mirrored in range(2):
            (kx, nx), (ky, ny), (kz, nz) = taps_of(v, 0), taps_of(v, 2), taps_of(v, 1)
            if mirrored:
                kx, ky, kz = kx[::-1], ky[::-1], kz[::-1]
            band_z = select(shift_z, kz, 0, 9) * (nx * nz)
            at_v = pl.ds(pl.multiple_of(v * 128, 128), 128)
            for s in range(3):
                block = select(shift_x + 4 * s, kx, max(4 * s - 3, 0), min(4 * s + 4, 9)) * band_z
                if mirrored:
                    flat[s] += jnp.broadcast_to(jnp.sum(block, axis=1, keepdims=True), flat.shape[1:])
                high, low = split(block)
                for part, value in enumerate((high, low, high)):
                    if mirrored:
                        column = pl.ds(pl.multiple_of(v * 384 + part * 128, 128), 128)
                        gather[pl.ds(256 - 128 * s, 128), column] = value
                    else:
                        spread[at_v, pl.ds(384 * s + 128 * part, 128)] = value
            lat = lat_b if mirrored else lat_f
            same = split(select(shift_y, ky, 0, 9) * ny)
            after = split(select(shift_y + 128, ky, 5, 9) * ny)
            before = split(select(shift_y - 128, ky, 0, 4) * ny)
            for part, which in enumerate((0, 1, 0)):
                for i in range(2):
                    for o in range(2):
                        at = pl.ds(256 * part + 128 * i, 128), pl.ds(128 * o, 128)
                        value = (same, after, before)[i - o][which]
                        lat[(v, 0) + at] = value
                        lat[(v, 1) + at] = zero if i == o else value
        return carry

    flat[...] = jnp.zeros_like(flat)
    lax.fori_loop(0, 4, build, 0)

    def put_parts(ref, base, value):
        high, low = split(value)
        ref[pl.ds(base, 128)] = high
        ref[pl.ds(base + 128, 128)] = high
        ref[pl.ds(base + 256, 128)] = low

    def three(high, low, at):
        return jnp.concatenate([high[:, at], high[:, at], low[:, at]], axis=1)

    def along_y(value, lat, v):
        high, low = split(value)
        halves = [three(high, low, slice(0, 256)), three(high, low, slice(256, 512))]
        inside = dot(jnp.concatenate(halves, axis=0), lat[v, 0])
        across = dot(three(high, low, slice(128, 384)), lat[v, 1])
        rows = value.shape[0]
        yield jnp.concatenate([inside[:rows, :128], inside[:rows, 128:] + across[:, :128]], axis=1)
        yield jnp.concatenate([inside[rows:, :128] + across[:, 128:], inside[rows:, 128:]], axis=1)

    def put_own(h):
        put_parts(dext, 384, est[h, pl.ds(0, 128)])
        put_parts(dext, 768, est[h, pl.ds(128, 128)])

    def put_halo(h):
        put_parts(dext, 0, halo[h, 0])
        put_parts(dext, 1152, halo[h, 1])

    def blur_all(h):
        put_own(h)
        put_halo(h)
        for i in range(2):
            first[i] = dot(spread[...], dext[pl.ds(384 * i, 1152)])

    def blur_early(h):
        put_own(h)
        for i in range(2):
            first[i] = dot(spread[:, pl.ds(384 - 384 * i, 768)], dext[pl.ds(384, 768)])
        wait_recv(halo_copy, h)
        put_halo(h)
        for i in range(2):
            first[i] += dot(spread[:, pl.ds(768 * i, 384)], dext[pl.ds(1152 * i, 384)])

    def sweep(h, send):
        def predict(v):
            at_v = pl.ds(v * 128, 128)
            value = jnp.concatenate([first[0, at_v], first[1, at_v]], axis=0)
            return list(along_y(value, lat_f, v))

        def divide(v, predicted):
            quotient = []
            for b in range(2):
                seen = data[h, v, :, pl.ds(256 * b, 256)].astype(F32)
                inverse = pl.reciprocal(predicted[b], approx=True)
                value = seen * inverse
                quotient.append(value + inverse * (seen - predicted[b] * value))
            return jnp.concatenate(quotient, axis=1)

        def spread_back(v, quotient):
            for b, corrected in enumerate(along_y(quotient, lat_b, v)):
                high, low = split(corrected)
                for part, piece in enumerate((high, high, low)):
                    at = pl.ds(v * 384 + 128 * part, 128)
                    for side in range(2):
                        cs[side, at, pl.ds(256 * b, 256)] = piece[128 * side : 128 * side + 128]

        predicted = predict(0)
        for v in range(4):
            following = predict(v + 1) if v < 3 else None
            spread_back(v, divide(v, predicted))
            predicted = following

        send(h)

    def gather_both(h):
        r0 = dot(gather[...], cs[0])
        corr_mine[h, 0] = r0[:128]
        corr_own[h] = r0[128:]
        r1 = dot(gather[...], cs[1])
        corr_mine[h, 1] = r1[256:]
        corr_own[h] += r1[:256]

    def wide(value):
        return jnp.concatenate([value] * (halo.shape[-1] // 128), axis=1)

    def flat_part(side):
        return wide(flat[0] if side == 0 else flat[2])

    def flat_own(side):
        return wide(flat[1] + (flat[2] if side == 0 else flat[0]))

    def send_both(h):
        gather_both(h)
        for side in range(2):
            both_out[h, side, pl.ds(0, 128)] = (corr_mine[h, side] - flat_part(1 - side)).astype(BF16)
            both_out[h, side, pl.ds(128, 128)] = (
                corr_own[h, pl.ds(128 * side, 128)] - flat_own(side)
            ).astype(BF16)
        start(both_copy, h)

    def send_last(h):
        for side in range(2):
            part = dot(gather[pl.ds(256 * side, 128)], cs[side])
            last_out[h, side] = (part - flat_part(1 - side)).astype(last_out.dtype)
        start(last_copy, h)
        corr_own[h] = dot(gather[pl.ds(128, 256)], cs[0])
        corr_own[h] += dot(gather[pl.ds(0, 256)], cs[1])

    def scale_own(h, side, received):
        at = pl.ds(128 * side, 128)
        near = has_left if side == 0 else has_right
        outside = jnp.where(near, flat_part(side) + received.astype(F32), 0.0)
        est[h, at] = est[h, at] * (0.25 * (corr_own[h, at] + outside))

    def update_both(h):
        wait_send(halo_copy, h)
        wait_recv(both_copy, h)
        for side in range(2):
            scale_own(h, side, both_in[h, side, pl.ds(0, 128)])
            theirs = flat_own(1 - side) + both_in[h, side, pl.ds(128, 128)].astype(F32)
            halo[h, side] = halo[h, side] * (0.25 * (corr_mine[h, side] + theirs))

    def update_last(h):
        wait_recv(last_copy, h)
        for side in range(2):
            scale_own(h, side, last_in[h, side])

    def spectrum(h):
        rows = dot(est[h].astype(BF16), table[...])
        lateral = rows.shape[1] // 2
        for g in range(2):
            at = slice(128 * g, 128 * g + 128)
            both = jnp.concatenate([rows[at, :lateral], rows[at, lateral:]], axis=0)
            high, low = split(both)
            spec[h, g] = dot(forward_z[...], jnp.concatenate([high, high, low], axis=0))

    for h in range(2):
        if h == 0:
            blur_early(h)
        else:
            wait_recv(halo_copy, h)
            blur_all(h)
        sweep(h, send_both)
    for h in range(2):
        update_both(h)
        blur_all(h)
        sweep(h, send_last)

    lateral = data.shape[3]
    half = depth // 2

    def power(a, b):
        total = jnp.zeros((depth, lateral), F32)
        for g in range(2):
            for at in range(0, 256, depth):
                total = total + spec[a, g, pl.ds(at, depth)] * spec[b, g, pl.ds(at, depth)]
        return total

    for copy in near[2:]:
        copy.wait()
    update_last(0)
    spectrum(0)
    power_0 = power(0, 0)

    ids = cycles[0, :, pl.ds(0, 256)].astype(F32)
    ids = jnp.concatenate([ids, jnp.zeros((128 - depth, 256), F32)], axis=0).T
    bins = lax.broadcasted_iota(jnp.int32, (256, CYCLES), 1).astype(F32)
    for k in range(depth // 2 + 1):
        onehot[pl.ds(256 * k, 256)] = jnp.where(bins == ids[:, k : k + 1], 1.0, 0.0).astype(BF16)

    update_last(1)
    spectrum(1)
    powers = (power(0, 1), power_0, power(1, 1))

    lane = lax.broadcasted_iota(jnp.int32, (1, 256), 1)
    weight_l = jnp.where(lane == 0, 1.0, 2.0)
    rows16 = lax.broadcasted_iota(jnp.int32, (half, 256), 0)
    edge = []
    cells = []
    for q, total in enumerate(powers):
        edge.append(jnp.sum(total[:, 256:257], axis=0, keepdims=True))
        low = total[:half, :256]
        high = total[half:, :256]
        pairs = (low + jnp.where(rows16 == 0, 0.0, high)) * weight_l
        last = high[:1] * weight_l
        cells.append([pairs[k : k + 1] for k in range(half)] + [high[:1] * weight_l])

    terms = []
    for k in range(half + 1):
        value = jnp.concatenate([cells[q][k] for q in range(3)] + [jnp.zeros((5, 256), F32)], axis=0)
        a = value.astype(BF16).astype(F32)
        b = (value - a).astype(BF16).astype(F32)
        terms.append(jnp.concatenate([a, b, value - a - b, jnp.zeros_like(a)], axis=0).astype(BF16))
    binned = dot(jnp.concatenate(terms, axis=1), onehot[...])
    binned = binned[0:8] + binned[8:16] + binned[16:24]
    bin_row = lax.broadcasted_iota(jnp.int32, (8, CYCLES), 0)
    bin_lane = lax.broadcasted_iota(jnp.int32, (8, CYCLES), 1)
    for q in range(3):
        binned = binned + jnp.where(
            (bin_row == q) & (bin_lane == CYCLES - 1), jnp.broadcast_to(edge[q], (8, CYCLES)), 0.0
        )
    red_out[...] = binned

    def share(step):
        peer = lax.rem(me + step, n)
        return pltpu.make_async_remote_copy(
            src_ref=red_out,
            dst_ref=red_in.at[step],
            send_sem=red_send.at[step],
            recv_sem=red_recv.at[step],
            device_id={"tile": peer},
            device_id_type=MESH,
        )

    def start_share(step, carry):
        share(step).start()
        return carry

    def wait_share(step, carry):
        share(step).wait()
        return carry + red_in[step]

    lax.fori_loop(1, n, start_share, 0)
    totals = lax.fori_loop(1, n, wait_share, binned)

    corr = totals[0:1] / (jnp.sqrt(totals[1:2]) * jnp.sqrt(totals[2:3]))
    scale = 0.5 / (depth * lateral)
    cycle_weight = jnp.where(lane <= cutoff[0], corr, 0.0) * scale
    low_table = jnp.broadcast_to(cycle_weight[:, :128], (8, 128))
    high_table = jnp.broadcast_to(cycle_weight[:, 128:], (8, 128))
    weights = []
    for r in range(0, half + 8, 8):
        pieces = []
        for c in range(0, lateral, 128):
            ids = cycles[0, pl.ds(r, 8), pl.ds(c, 128)]
            index = ids & 127
            from_low = jnp.take_along_axis(low_table, index, axis=1)
            from_high = jnp.take_along_axis(high_table, index, axis=1)
            pieces.append(jnp.where(ids < 128, from_low, from_high))
        weights.append(jnp.concatenate(pieces, axis=1))
    low = jnp.concatenate(weights[:-1], axis=0)
    row0 = lax.broadcasted_iota(jnp.int32, (half, lateral), 0) == 0
    high = jnp.where(row0, jnp.broadcast_to(weights[-1][0:1], (half, lateral)), low)
    cell = jnp.concatenate([low, high], axis=0)

    for g in range(2):
        mixed = jnp.concatenate(
            [
                (spec[0, g, pl.ds(at, depth)] + spec[1, g, pl.ds(at, depth)]) * cell
                for at in range(0, 256, depth)
            ],
            axis=0,
        )
        high, low = split(mixed)
        inner = dot(inverse_z[...], jnp.concatenate([high, high, low], axis=0)).astype(BF16)
        out[pl.ds(128 * g, 128)] = dot(inner[:128], table[:, pl.ds(0, lateral)]) + dot(
            inner[128:], table[:, pl.ds(lateral, lateral)]
        )

    for h in range(2):
        wait_send(both_copy, h)
        wait_send(last_copy, h)


def body(data_halves, psf_taps, cycle_map, cutoff):
    halves, views, slab, depth, lateral = data_halves.shape
    n = lax.axis_size("tile")
    rows = slab * depth
    table, forward_z, inverse_z = constants(depth, lateral)
    vmem = pl.BlockSpec(memory_space=pltpu.VMEM)
    smem = pl.BlockSpec(memory_space=pltpu.SMEM)
    far = pl.BlockSpec(memory_space=pl.ANY)
    dma = pltpu.SemaphoreType.DMA
    joined = pl.pallas_call(
        functools.partial(kernel, n),
        out_shape=jax.ShapeDtypeStruct((rows, lateral), F32),
        in_specs=[far, smem, vmem, smem, far, far, far],
        out_specs=vmem,
        scratch_shapes=[
            pltpu.VMEM((halves, views, rows, lateral), BF16),
            pltpu.VMEM(table.shape, BF16),
            pltpu.VMEM(forward_z.shape, BF16),
            pltpu.VMEM(inverse_z.shape, BF16),
            dma((5,)),
            pltpu.VMEM((2, rows, lateral), F32),
            pltpu.VMEM((2, 2, 128, lateral), F32),
            pltpu.VMEM((2, 2, 128, lateral), F32),
            pltpu.VMEM((2, rows, lateral), F32),
            pltpu.VMEM((3, 128, 128), F32),
            pltpu.VMEM((2, 2, 256, lateral), BF16),
            pltpu.VMEM((2, 2, 256, lateral), BF16),
            pltpu.VMEM((2, 2, 128, lateral), BF16),
            pltpu.VMEM((2, 2, 128, lateral), BF16),
            pltpu.VMEM((512, 1152), BF16),
            pltpu.VMEM((384, 1536), BF16),
            pltpu.VMEM((4, 2, 768, 256), BF16),
            pltpu.VMEM((4, 2, 768, 256), BF16),
            pltpu.VMEM((1536, lateral), BF16),
            pltpu.VMEM((2, 512, lateral), F32),
            pltpu.VMEM((2, 1536, lateral), BF16),
            pltpu.VMEM(((depth // 2 + 1) * 256, CYCLES), BF16),
            pltpu.VMEM((2, 2, rows, lateral), F32),
            pltpu.VMEM((8, CYCLES), F32),
            pltpu.VMEM((n, 8, CYCLES), F32),
            dma((2, 2)),
            dma((2, 2)),
            dma((2, 2)),
            dma((2, 2)),
            dma((2, 2)),
            dma((2, 2)),
            dma((n,)),
            dma((n,)),
        ],
        compiler_params=pltpu.CompilerParams(
            collective_id=0, has_side_effects=True, vmem_limit_bytes=56 * 1024 * 1024
        ),
    )(
        data_halves.reshape(halves, views, rows, lateral),
        jnp.transpose(psf_taps, (1, 0, 2)),
        cycle_map,
        cutoff,
        jnp.asarray(table),
        jnp.asarray(forward_z),
        jnp.asarray(inverse_z),
    )
    return joined.reshape(slab, depth, lateral)


def solution(mesh):
    in_specs = (
        P(None, None, ("groups", "tile"), None, None),
        P(),
        P(("groups", "tile"), None, None),
        P("groups"),
    )
    out_specs = P(("groups", "tile"), None, None)
    return jax.shard_map(body, mesh=mesh, in_specs=in_specs, out_specs=out_specs, check_vma=False)
```
